256 devices in a mesh: dp: 32 (over z, y), tensor: 8 (over x, core).
Axes of the slice: x: 4, y: 4, z: 8, core: 2. Of those that a mesh axis runs over, the one named last changes fastest.
Arguments:
- inputs: bfloat16 [32768, 8192], P(('dp', 'tensor')), may hold values from -6 to 6
- out_grads: bfloat16 [32768, 2048], P('dp', 'tensor'), may hold values from -0.1875 to 0.1875
- error_in: bfloat16 [32, 8192, 2048], P('dp', None, 'tensor'), may hold values from -6 to 6
- basis_in: float32 [2048, 128], P('tensor'), may hold values from -6 to 6
Outputs:
- rebuilt: bfloat16 [8192, 2048], P('dp', 'tensor')
- error_out: bfloat16 [32, 8192, 2048], P('dp', None, 'tensor')
- basis_out: float32 [2048, 128], P('tensor')
The draws below stay inside these ranges and needn't reach their ends.
All inputs are finite; a program needn't handle non-finite values.
Results may differ from the reference program's by a relative error of at most 0.0024.
Values may be sent and summed in bfloat16 or wider, within the bound.
A program may use at most 128 MiB of HBM per device.

```python
import jax
import jax.numpy as jnp
from jax import lax

D = 8192
KV = 2048
RANK = 128
TOK_REP = 1024
REPLICAS = 32
TOKENS = 32768


def steps_of(key, dims, pieces, least, top_value):
    gain, own = 1.0, jax.random.fold_in(key, 6)
    for dim, blocks in pieces:
        draws = jnp.exp(jax.random.uniform(jax.random.fold_in(own, dim), (blocks,), jnp.float32, least / len(pieces), top_value / len(pieces)))
        gain = gain * jnp.repeat(draws, dims[dim] // blocks).reshape([-1 if axis == dim else 1 for axis in range(len(dims))])
    return gain


def centred(key, extent, deviation, bound, split=(), held_as=jnp.bfloat16):
    factor_of = steps_of(key, extent, split, -0.22, 0.18) if split else 1.0
    array = jax.random.normal(key, extent, jnp.float32) * deviation * factor_of
    return jnp.minimum(jnp.maximum(array, -bound), bound).astype(held_as)


def setup_inputs(seed: int = 0) -> dict:
    splits = jax.random.split(jax.random.key(seed), 5)
    return {
        "inputs": centred(splits[0], (TOKENS, D), 1.0, 6.0, ((0, 256),)),
        "out_grads": centred(splits[1], (TOKENS, KV), TOK_REP ** -0.5, 0.1875, ((0, 32), (1, 8))),
        "error_in": centred(splits[2], (REPLICAS, D, KV), 1.0, 6.0, ((0, 32), (2, 8))),
        "basis_in": centred(splits[3], (KV, RANK), 1.0, 6.0, ((0, 8),), jnp.float32),
    }


highest = lax.Precision.HIGHEST

def right_solve(lower, values):
    return lax.linalg.triangular_solve(lower, values, left_side=False, lower=True, transpose_a=True)

def reference(inputs, out_grads, error_in, basis_in):
    tokens_in = inputs.reshape(REPLICAS, TOK_REP, D)
    grads_in = out_grads.reshape(REPLICAS, TOK_REP, KV)

    def merge_one(index):
        gradient = lax.dot_general(tokens_in[index].astype(jnp.float32), grads_in[index].astype(jnp.float32), (((0,), (0,)), ((), ())), preferred_element_type=jnp.float32)
        return gradient + error_in[index].astype(jnp.float32)
    merged = lax.map(merge_one, jnp.arange(REPLICAS, dtype=jnp.int32))
    low_rank = jnp.einsum('rdk,kj->dj', merged, basis_in, precision=highest) / REPLICAS
    gram = jnp.dot(low_rank.T, low_rank, precision=highest)
    lower = jnp.linalg.cholesky(gram)
    ortho = right_solve(lower, low_rank)
    basis_out = jnp.einsum('rdk,dj->kj', merged, ortho, precision=highest) / REPLICAS
    rebuilt_full = jnp.dot(ortho, basis_out.T, precision=highest)
    error_out = (merged - rebuilt_full[None]).astype(jnp.bfloat16)
    return (rebuilt_full.astype(jnp.bfloat16), error_out, basis_out)
```

```python
import functools

import jax
import jax.numpy as jnp
from jax import lax
from jax.experimental import pallas as pl
from jax.experimental.pallas import tpu as pltpu
from jax.sharding import PartitionSpec as P

NX = 4
NY = 4
RANK = 128
NCH = 4
XCH = 8
f32, bf16 = jnp.float32, jnp.bfloat16
MESH = pl.DeviceIdType.MESH
OVER_ROWS = (((0,), (0,)), ((), ()))


def split(value):
    high = value.astype(bf16)
    return high, (value - high.astype(f32)).astype(bf16)


def split_columns(value):
    return jnp.concatenate(split(value), axis=1)


def rows_dot(left, right, **kw):
    return lax.dot_general(left, right, OVER_ROWS, preferred_element_type=f32, **kw)


def dot(left, right, **kw):
    return jnp.dot(left, right, preferred_element_type=f32, **kw)


def exchange(
    nz, scale,
    x_hbm, g_hbm, e_hbm, basis,
    merged_hbm, lr_hbm, wt_ref, bt_ref,
    xg, g, e, p, d2d, yb, zb, xb, lr, merged,
    gb, gbd, gbx, bhl, gbhl,
    yt, yz, yy, yr, gram, aug,
    local, gb_s, gb_r, x_s, x_r, f_s, f_r, sib_s, sib_r,
    d_s, d_r, y_s, y_r, z_s, z_r, xx_s, xx_r,
    za_s, za_r, ya_s, ya_r, da_s, da_r,
    q_s, q_r, out_sem,
):
    width = x_hbm.shape[1]
    tok = x_hbm.shape[0]
    cols = e.shape[1]
    half = width // 2
    hc = half // NCH
    ybl = hc // NY
    zbl = ybl // nz
    cw = width // XCH
    dp = lax.axis_index("dp")
    t = lax.axis_index("tensor")
    z, y = dp // NY, dp % NY
    x, c = t // 2, t % 2
    sib = (dp, x * 2 + (1 - c))

    def at_x(o):
        return lax.rem(x + o + NX, NX)

    def to_x(o):
        return (dp, at_x(o) * 2 + c)

    def at_y(o):
        return lax.rem(y + o, NY)

    def to_y(o):
        return (z * NY + at_y(o), t)

    def at_z(o):
        return lax.rem(z + o, nz)

    def to_z(o):
        return (at_z(o) * NY + y, t)

    sent = []

    def send(src, dst, send_sem, recv_sem, device):
        copy = pltpu.make_async_remote_copy(
            src_ref=src, dst_ref=dst, send_sem=send_sem, recv_sem=recv_sem,
            device_id=device, device_id_type=MESH,
        )
        copy.start()
        sent.append(copy)
        return copy

    load_g = pltpu.make_async_copy(g_hbm, g, local.at[0])
    load_x = pltpu.make_async_copy(x_hbm, xg.at[t], local.at[1])
    load_e = pltpu.make_async_copy(e_hbm, e, local.at[2])
    load_g.start()
    load_x.start()
    load_e.start()

    barrier = pltpu.get_barrier_semaphore()
    partners = [sib] + [to_x(o) for o in range(1, NX)] + [to_y(o) for o in range(1, NY)] + [to_z(o) for o in range(1, nz)]
    for device in partners:
        pl.semaphore_signal(barrier, inc=1, device_id=device, device_id_type=MESH)

    bhl[...] = split_columns(basis[...])
    load_g.wait()
    for block in range(2 * NX):
        product = dot(g[block * tok:(block + 1) * tok, :], bhl[...])
        gb[block % 2, block // 2] = product[:, :RANK] + product[:, RANK:]
    pl.semaphore_wait(barrier, len(partners))
    gb_copy = send(gb.at[1 - c], gbd, gb_s.at[0], gb_r.at[0], sib)
    load_x.wait()
    gb_copy.wait_recv()
    gb[c] = gb[c] + gbd[...]
    gb_copies = [
        send(gb.at[c, at_x(o)], gbx.at[o - 1], gb_s.at[o], gb_r.at[o], to_x(o)) for o in range(1, NX)
    ]

    def chunk_of(shard, j):
        return xg.at[shard, :, pl.ds(j * cw, cw)]

    ring = []
    for j in range(XCH):
        ring.append([
            send(chunk_of(t, j), chunk_of(t, j), x_s.at[j, i], x_r.at[j, i], to_x(o))
            for i, o in enumerate((1, -1))
        ])
    own_sib = send(xg.at[t], xg.at[t], sib_s.at[XCH, 0], sib_r.at[XCH, 0], sib)

    far = [None] * XCH
    to_sib = [[] for _ in range(XCH)]

    def near(j):
        ring[j][0].wait_recv()
        ring[j][1].wait_recv()
        left = chunk_of(at_x(-1) * 2 + c, j)
        right = chunk_of(at_x(1) * 2 + c, j)
        if j % 2 == 0:
            far[j] = send(left, left, f_s.at[j], f_r.at[j], to_x(1))
        else:
            far[j] = send(right, right, f_s.at[j], f_r.at[j], to_x(-1))
        to_sib[j].append(send(left, left, sib_s.at[j, 0], sib_r.at[j, 0], sib))
        to_sib[j].append(send(right, right, sib_s.at[j, 1], sib_r.at[j, 1], sib))

    def distant(j):
        far[j].wait_recv()
        block = chunk_of(at_x(2) * 2 + c, j)
        to_sib[j].append(send(block, block, sib_s.at[j, 2], sib_r.at[j, 2], sib))

    merged_copies = []

    def multiply(j):
        if j == 0:
            own_sib.wait_recv()
        for copy in to_sib[j]:
            copy.wait_recv()
        tile = min(256, cw)

        @pl.loop(0, cw // tile)
        def _(i):
            row = pl.multiple_of(j * cw + i * tile, tile)
            block = xg[:, :, pl.ds(row, tile)].reshape(2 * NX * tok, tile)
            merged[pl.ds(row, tile), :] = rows_dot(block, g[...]) + e[pl.ds(row, tile), :].astype(f32)

        copy = pltpu.make_async_copy(
            merged.at[pl.ds(j * cw, cw)], merged_hbm.at[pl.ds(j * cw, cw)], out_sem.at[j])
        copy.start()
        merged_copies.append(copy)

    for copy in gb_copies:
        copy.wait_recv()
    gbhl[...] = split_columns(gb[c, x] + gbx[0] + gbx[1] + gbx[2])
    load_e.wait()

    def partial(h, k):
        tile = min(512, hc)

        @pl.loop(0, hc // tile)
        def _(i):
            at = pl.multiple_of(k * hc + i * tile, tile)
            row = pl.multiple_of(h * half + at, tile)
            total = rows_dot(xg[t, :, pl.ds(row, tile)], gbhl[...]) + dot(e[pl.ds(row, tile), :], bhl[...])
            p[h, pl.ds(at, tile), :] = total[:, :RANK] + total[:, RANK:]

    y_copies, z_copies, x_copies = {}, {}, {}
    za_copies, ya_copies, da_copies = {}, {}, {}
    for k in range(NCH):
        partial(1 - c, k)
        rows = pl.ds(k * hc, hc)
        d_copy = send(p.at[1 - c, rows], d2d.at[rows], d_s.at[k], d_r.at[k], sib)
        partial(c, k)
        d_copy.wait_recv()
        p[c, rows, :] = p[c, rows, :] + d2d[rows, :]
        y_copies[k] = [
            send(p.at[c, pl.ds(k * hc + at_y(o) * ybl, ybl)], yb.at[k, o - 1], y_s.at[k, o - 1], y_r.at[k, o - 1], to_y(o))
            for o in range(1, NY)
        ]

    def own_y(k):
        return pl.ds(pl.multiple_of(k * hc + y * ybl, ybl), ybl)

    def own_z(k):
        return pl.ds(pl.multiple_of(k * hc + y * ybl + z * zbl, zbl), zbl)

    def stage_y(k):
        for copy in y_copies[k]:
            copy.wait_recv()
        total = p[c, own_y(k), :]
        for i in range(NY - 1):
            total = total + yb[k, i]
        p[c, own_y(k), :] = total
        z_copies[k] = [
            send(p.at[c, pl.ds(pl.multiple_of(k * hc + y * ybl + at_z(o) * zbl, zbl), zbl)], zb.at[k, o - 1],
                 z_s.at[k, o - 1], z_r.at[k, o - 1], to_z(o))
            for o in range(1, nz)
        ]

    def stage_z(k):
        for copy in z_copies[k]:
            copy.wait_recv()
        total = p[c, own_z(k), :]
        for i in range(nz - 1):
            total = total + zb[k, i]
        xb[k, x] = total
        x_copies[k] = [
            send(xb.at[k, x], xb.at[k, x], xx_s.at[k, o - 1], xx_r.at[k, o - 1], to_x(o)) for o in range(1, NX)
        ]

    def stage_x(k):
        for copy in x_copies[k]:
            copy.wait_recv()
        total = xb[k, 0]
        for i in range(1, NX):
            total = total + xb[k, i]
        lr[c, own_z(k), :] = split_columns(total * scale)
        block = lr.at[c, own_z(k)]
        za_copies[k] = [
            send(block, block, za_s.at[k, o - 1], za_r.at[k, o - 1], to_z(o)) for o in range(1, nz)
        ]

    def gather_z(k):
        for copy in za_copies[k]:
            copy.wait_recv()
        block = lr.at[c, own_y(k)]
        ya_copies[k] = [
            send(block, block, ya_s.at[k, o - 1], ya_r.at[k, o - 1], to_y(o)) for o in range(1, NY)
        ]

    def gather_y(k):
        for copy in ya_copies[k]:
            copy.wait_recv()
        block = lr.at[c, pl.ds(k * hc, hc)]
        da_copies[k] = send(block, block, da_s.at[k], da_r.at[k], sib)

    lr_copies = []

    def gather_core(k):
        da_copies[k].wait_recv()
        for h in range(2):
            copy = pltpu.make_async_copy(
                lr.at[h, pl.ds(k * hc, hc)], lr_hbm.at[pl.ds(h * half + k * hc, hc)], out_sem.at[XCH + 2 * k + h])
            copy.start()
            lr_copies.append(copy)

    def right(h, k):
        tile = min(512, hc)

        @pl.loop(0, hc // tile)
        def _(i):
            at = pl.multiple_of(k * hc + i * tile, tile)
            pair = lr[h, pl.ds(at, tile), :]
            high, low = split(merged[pl.ds(pl.multiple_of(h * half + at, tile), tile), :])
            both = rows_dot(pair, high)
            yt[...] += both[:RANK] + both[RANK:] + rows_dot(pair[:, :RANK], low)
            square = rows_dot(pair, pair)
            gram[...] += (square[:RANK, :RANK] + square[RANK:, RANK:]) + (square[:RANK, RANK:] + square[RANK:, :RANK])

    yt[...] = jnp.zeros_like(yt)
    gram[...] = jnp.zeros_like(gram)
    stages = (stage_y, stage_z, stage_x, gather_z, gather_y, gather_core)
    for s in range(NCH + len(stages) - 1):
        for lag, stage in enumerate(stages):
            if 0 <= s - lag < NCH:
                stage(s - lag)
        if s < XCH:
            near(s)
    for j in range(XCH):
        distant(j)
    for j in range(XCH):
        multiply(j)
    for h in range(2):
        for k in range(NCH):
            right(h, k)

    lane = lax.broadcasted_iota(jnp.int32, (RANK, 2 * RANK), 1)
    sub = lax.broadcasted_iota(jnp.int32, (RANK, 2 * RANK), 0)
    aug[:, :RANK] = gram[...]
    aug[:, RANK:] = jnp.where(
        lax.broadcasted_iota(jnp.int32, (RANK, RANK), 0) == lax.broadcasted_iota(jnp.int32, (RANK, RANK), 1), 1.0, 0.0)

    def eliminate(first, last):
        @pl.loop(first, last)
        def _(j):
            row = aug[pl.ds(j, 1), :]
            pivot = jnp.sum(jnp.where(lane[:1] == j, row, 0.0), axis=1, keepdims=True)
            column = jnp.sum(jnp.where(lane == j, aug[...], 0.0), axis=1, keepdims=True)
            factor = jnp.where(sub[:, :1] > j, column / pivot, 0.0)
            aug[...] = aug[...] - factor * row

    part = RANK // nz
    own = pl.ds(pl.multiple_of(z * part, part), part)
    cuts = (0, RANK // 3, 2 * RANK // 3, RANK)
    copies = [
        send(yt.at[pl.ds(pl.multiple_of(at_z(o) * part, part), part)], yz.at[o - 1], q_s.at[0, o - 1], q_r.at[0, o - 1], to_z(o))
        for o in range(1, nz)
    ]
    eliminate(cuts[0], cuts[1])
    for copy in copies:
        copy.wait_recv()
    total = yt[own, :]
    for i in range(nz - 1):
        total = total + yz[i]
    yy[y] = total
    copies = [send(yy.at[y], yy.at[y], q_s.at[1, o - 1], q_r.at[1, o - 1], to_y(o)) for o in range(1, NY)]
    eliminate(cuts[1], cuts[2])
    for copy in copies:
        copy.wait_recv()
    total = yy[0]
    for i in range(1, NY):
        total = total + yy[i]
    yr[own, :] = total * scale
    copies = [send(yr.at[own], yr.at[own], q_s.at[2, o - 1], q_r.at[2, o - 1], to_z(o)) for o in range(1, nz)]
    eliminate(cuts[2], cuts[3])
    pivots = jnp.sum(jnp.where(lane == sub, aug[...], 0.0), axis=1, keepdims=True)
    inverse = aug[:, RANK:] / jnp.sqrt(pivots)
    for copy in copies:
        copy.wait_recv()
    bt = dot(inverse, yr[...], precision=lax.Precision.HIGHEST)
    bt_ref[...] = bt
    wt_ref[...] = rows_dot(inverse, bt, precision=lax.Precision.HIGHEST)
    for copy in sent:
        copy.wait_send()
    for copy in merged_copies + lr_copies:
        copy.wait()


def finish(index, merged, lr, lr_own, wt, bt, rebuilt_ref, error_ref, basis_ref):
    high, low = split(wt[...])
    twice = jnp.concatenate([high, high], axis=0)

    def rebuild(pair):
        return dot(pair, twice) + dot(pair[:, :RANK], low)

    error_ref[0] = (merged[...] - rebuild(lr[...])).astype(bf16)

    @pl.when(pl.program_id(0) == 0)
    def _():
        rebuilt_ref[...] = rebuild(lr_own[...]).astype(bf16)
        basis_ref[...] = bt[...].T


def shards(inputs, out_grads, error_in, basis_in):
    replicas = lax.axis_size("dp")
    nz = replicas // NY
    tok, width = inputs.shape
    tokens, cols = out_grads.shape
    half = width // 2
    hc = half // NCH
    ybl = hc // NY
    zbl = ybl // nz
    scratch = [
        ((2 * NX, tok, width), bf16),
        ((tokens, cols), bf16),
        ((width, cols), bf16),
        ((2, half, RANK), f32),
        ((half, RANK), f32),
        ((NCH, NY - 1, ybl, RANK), f32),
        ((NCH, nz - 1, zbl, RANK), f32),
        ((NCH, NX, zbl, RANK), f32),
        ((2, half, 2 * RANK), bf16),
        ((width, cols), f32),
        ((2, NX, tok, RANK), f32),
        ((NX, tok, RANK), f32),
        ((NX - 1, tok, RANK), f32),
        ((cols, 2 * RANK), bf16),
        ((tok, 2 * RANK), bf16),
        ((RANK, cols), f32),
        ((nz - 1, RANK // nz, cols), f32),
        ((NY, RANK // nz, cols), f32),
        ((RANK, cols), f32),
        ((RANK, RANK), f32),
        ((RANK, 2 * RANK), f32),
    ]
    sems = [
        (3,), (NX,), (NX,), (XCH, 2), (XCH, 2), (XCH,), (XCH,), (XCH + 1, 3), (XCH + 1, 3),
        (NCH,), (NCH,), (NCH, NY - 1), (NCH, NY - 1), (NCH, nz - 1), (NCH, nz - 1), (NCH, NX - 1), (NCH, NX - 1),
        (NCH, nz - 1), (NCH, nz - 1), (NCH, NY - 1), (NCH, NY - 1), (NCH,), (NCH,),
        (3, nz), (3, nz), (XCH + 2 * NCH,),
    ]
    anywhere = pl.BlockSpec(memory_space=pl.ANY)
    vmem = pl.BlockSpec(memory_space=pltpu.VMEM)
    merged, lr, wt, bt = pl.pallas_call(
        functools.partial(exchange, nz, 1.0 / replicas),
        out_shape=(
            jax.ShapeDtypeStruct((width, cols), f32),
            jax.ShapeDtypeStruct((width, 2 * RANK), bf16),
            jax.ShapeDtypeStruct((RANK, cols), f32),
            jax.ShapeDtypeStruct((RANK, cols), f32),
        ),
        in_specs=[anywhere, anywhere, anywhere, vmem],
        out_specs=(anywhere, anywhere, vmem, vmem),
        scratch_shapes=[pltpu.VMEM(s, d) for s, d in scratch] + [pltpu.SemaphoreType.DMA(s) for s in sems],
        compiler_params=pltpu.CompilerParams(
            collective_id=0, has_side_effects=True, vmem_limit_bytes=60 * 2**20),
        name="exchange",
    )(inputs, out_grads, error_in[0], basis_in)

    block = width // 8
    share = width // replicas
    index = lax.axis_index("dp").astype(jnp.int32).reshape(1)
    whole = lambda i, s: (0, 0)
    rows = lambda i, s: (i, 0)
    rebuilt, error_out, basis = pl.pallas_call(
        finish,
        out_shape=(
            jax.ShapeDtypeStruct((share, cols), bf16),
            jax.ShapeDtypeStruct((1, width, cols), bf16),
            jax.ShapeDtypeStruct((cols, RANK), f32),
        ),
        grid_spec=pltpu.PrefetchScalarGridSpec(
            num_scalar_prefetch=1,
            grid=(width // block,),
            in_specs=[
                pl.BlockSpec((block, cols), rows),
                pl.BlockSpec((block, 2 * RANK), rows),
                pl.BlockSpec((share, 2 * RANK), lambda i, s: (s[0], 0)),
                pl.BlockSpec((RANK, cols), whole),
                pl.BlockSpec((RANK, cols), whole),
            ],
            out_specs=(
                pl.BlockSpec((share, cols), whole),
                pl.BlockSpec((1, block, cols), lambda i, s: (0, i, 0)),
                pl.BlockSpec((cols, RANK), whole),
            ),
        ),
        name="finish",
    )(index, merged, lr, lr, wt, bt)
    return rebuilt, error_out, basis


def solution(mesh):
    placed = (
        P(("dp", "tensor"), None),
        P("dp", "tensor"),
        P("dp", None, "tensor"),
        P("tensor", None),
    )
    return jax.shard_map(
        shards,
        mesh=mesh,
        in_specs=placed,
        out_specs=(P("dp", "tensor"), P("dp", None, "tensor"), P("tensor", None)),
        check_vma=False,
    )
```

```python
import functools

import jax
import jax.numpy as jnp
from jax import lax
from jax.experimental import pallas as pl
from jax.experimental.pallas import tpu as pltpu
from jax.sharding import PartitionSpec as P

NX = 4
NY = 4
RANK = 128
NCH = 4
XCH = 16
LAG = 6
OUT = 8
f32, bf16 = jnp.float32, jnp.bfloat16
MESH = pl.DeviceIdType.MESH
OVER_ROWS = (((0,), (0,)), ((), ()))


def split(value):
    high = value.astype(bf16)
    return high, (value - high.astype(f32)).astype(bf16)


def split_columns(value):
    return jnp.concatenate(split(value), axis=1)


def rows_dot(left, right, **kw):
    return lax.dot_general(left, right, OVER_ROWS, preferred_element_type=f32, **kw)


def dot(left, right, **kw):
    return jnp.dot(left, right, preferred_element_type=f32, **kw)


def exchange(
    nz, scale,
    x_hbm, g_hbm, e_hbm, basis,
    merged, lr, wt_ref, bt_ref,
    xg, g, e, p, d2d, yb, zb, xb,
    gb, gbd, gbx, bhl, gbhl,
    u, ub, yt, yb2, yy, yr, gram, aug,
    local, gb_s, gb_r, x_s, x_r, f_s, f_r, sib_s, sib_r,
    d_s, d_r, y_s, y_r, z_s, z_r, xx_s, xx_r,
    za_s, za_r, ya_s, ya_r, da_s, da_r,
    u_s, u_r, q_s, q_r,
):
    width = x_hbm.shape[1]
    tok = x_hbm.shape[0]
    cols = e.shape[1]
    half = width // 2
    hc = half // NCH
    ybl = hc // NY
    zbl = ybl // nz
    cw = width // XCH
    dp = lax.axis_index("dp")
    t = lax.axis_index("tensor")
    z, y = dp // NY, dp % NY
    x, c = t // 2, t % 2
    sib = (dp, x * 2 + (1 - c))

    def at_x(o):
        return lax.rem(x + o + NX, NX)

    def to_x(o):
        return (dp, at_x(o) * 2 + c)

    def at_y(o):
        return lax.rem(y + o, NY)

    def to_y(o):
        return (z * NY + at_y(o), t)

    def at_z(o):
        return lax.rem(z + o, nz)

    def to_z(o):
        return (at_z(o) * NY + y, t)

    sent = []

    def send(src, dst, send_sem, recv_sem, device):
        copy = pltpu.make_async_remote_copy(
            src_ref=src, dst_ref=dst, send_sem=send_sem, recv_sem=recv_sem,
            device_id=device, device_id_type=MESH,
        )
        copy.start()
        sent.append(copy)
        return copy

    load_g = pltpu.make_async_copy(g_hbm, g, local.at[0])
    load_x = pltpu.make_async_copy(x_hbm, xg.at[t], local.at[1])
    load_e = pltpu.make_async_copy(e_hbm, e, local.at[2])
    load_g.start()
    load_x.start()
    load_e.start()

    barrier = pltpu.get_barrier_semaphore()
    partners = [sib] + [to_x(o) for o in range(1, NX)] + [to_y(o) for o in range(1, NY)] + [to_z(o) for o in range(1, nz)]
    for device in partners:
        pl.semaphore_signal(barrier, inc=1, device_id=device, device_id_type=MESH)

    bhl[...] = split_columns(basis[...])
    load_g.wait()
    for block in range(2 * NX):
        product = dot(g[block * tok:(block + 1) * tok, :], bhl[...])
        gb[block % 2, block // 2] = product[:, :RANK] + product[:, RANK:]
    pl.semaphore_wait(barrier, len(partners))
    gb_copy = send(gb.at[1 - c], gbd, gb_s.at[0], gb_r.at[0], sib)
    load_x.wait()

    def chunk_of(shard, j):
        return xg.at[shard, :, pl.ds(j * cw, cw)]

    def own_chunk(j):
        return [
            send(chunk_of(t, j), chunk_of(t, j), x_s.at[j, i], x_r.at[j, i], to_x(o))
            for i, o in enumerate((1, -1))
        ]

    ring = []
    far = [None] * XCH
    to_sib = [[] for _ in range(XCH)]

    def near(j):
        ring[j][0].wait_recv()
        ring[j][1].wait_recv()
        left = chunk_of(at_x(-1) * 2 + c, j)
        right = chunk_of(at_x(1) * 2 + c, j)
        first, last = pl.ds(0, tok // 2), pl.ds(tok // 2, tok // 2)
        far[j] = [
            send(left.at[first], left.at[first], f_s.at[j, 0], f_r.at[j, 0], to_x(1)),
            send(right.at[last], right.at[last], f_s.at[j, 1], f_r.at[j, 1], to_x(-1)),
        ]
        to_sib[j].append(send(left, left, sib_s.at[j, 0], sib_r.at[j, 0], sib))
        to_sib[j].append(send(right, right, sib_s.at[j, 1], sib_r.at[j, 1], sib))

    todo = []
    for j in range(XCH + LAG):
        if j < XCH:
            todo.append(functools.partial(lambda j: ring.append(own_chunk(j)), j))
        if j >= LAG:
            todo.append(functools.partial(near, j - LAG))

    def pump(count=1):
        for _ in range(count):
            if todo:
                todo.pop(0)()

    pump(2)
    gb_copy.wait_recv()
    gb[c] = gb[c] + gbd[...]
    gb_copies = [
        send(gb.at[c, at_x(o)], gbx.at[o - 1], gb_s.at[o], gb_r.at[o], to_x(o)) for o in range(1, NX)
    ]

    own_sib = send(xg.at[t], xg.at[t], sib_s.at[XCH, 0], sib_r.at[XCH, 0], sib)
    pump(2)

    def distant(j):
        for copy in far[j]:
            copy.wait_recv()
        block = chunk_of(at_x(2) * 2 + c, j)
        to_sib[j].append(send(block, block, sib_s.at[j, 2], sib_r.at[j, 2], sib))

    def multiply(j):
        if j == 0:
            own_sib.wait_recv()
        for copy in to_sib[j]:
            copy.wait_recv()
        tile = min(256, cw)

        @pl.loop(0, cw // tile)
        def _(i):
            row = pl.multiple_of(j * cw + i * tile, tile)
            block = xg[:, :, pl.ds(row, tile)].reshape(2 * NX * tok, tile)
            merged[pl.ds(row, tile), :] = rows_dot(block, g[...]) + e[pl.ds(row, tile), :].astype(f32)

    load_e.wait()
    base = min(512, width)

    @pl.loop(0, width // base)
    def _(i):
        row = pl.multiple_of(i * base, base)
        total = dot(e[pl.ds(row, base), :], bhl[...])
        p[pl.ds(row, base), :] = total[:, :RANK] + total[:, RANK:]

    for copy in gb_copies:
        copy.wait_recv()
    gbhl[...] = split_columns(gb[c, x] + gbx[0] + gbx[1] + gbx[2])

    def partial(h, k):
        tile = min(512, hc)

        @pl.loop(0, hc // tile)
        def _(i):
            at = pl.multiple_of(k * hc + i * tile, tile)
            row = pl.multiple_of(h * half + at, tile)
            total = rows_dot(xg[t, :, pl.ds(row, tile)], gbhl[...])
            p[pl.ds(row, tile), :] += total[:, :RANK] + total[:, RANK:]

    def mine(start, size):
        return pl.ds(pl.multiple_of(c * half + start, size), size)

    def theirs(start, size):
        return pl.ds(pl.multiple_of((1 - c) * half + start, size), size)

    y_copies, z_copies, x_copies = {}, {}, {}
    za_copies, ya_copies, da_copies = {}, {}, {}
    d_copies = {}

    def feed_core(k):
        partial(1 - c, k)
        d_copies[k] = send(p.at[theirs(k * hc, hc)], d2d.at[pl.ds(k * hc, hc)], d_s.at[k], d_r.at[k], sib)
        partial(c, k)

    def feed_y(k):
        d_copies[k].wait_recv()
        p[mine(k * hc, hc), :] += d2d[pl.ds(k * hc, hc), :]
        y_copies[k] = [
            send(p.at[mine(k * hc + at_y(o) * ybl, ybl)], yb.at[k, o - 1], y_s.at[k, o - 1], y_r.at[k, o - 1], to_y(o))
            for o in range(1, NY)
        ]

    def own_y(k):
        return mine(k * hc + y * ybl, ybl)

    def own_z(k):
        return mine(k * hc + y * ybl + z * zbl, zbl)

    def stage_y(k):
        for copy in y_copies[k]:
            copy.wait_recv()
        total = p[own_y(k), :]
        for i in range(NY - 1):
            total = total + yb[k, i]
        p[own_y(k), :] = total
        z_copies[k] = [
            send(p.at[mine(k * hc + y * ybl + at_z(o) * zbl, zbl)], zb.at[k, o - 1],
                 z_s.at[k, o - 1], z_r.at[k, o - 1], to_z(o))
            for o in range(1, nz)
        ]

    def stage_z(k):
        for copy in z_copies[k]:
            copy.wait_recv()
        total = p[own_z(k), :]
        for i in range(nz - 1):
            total = total + zb[k, i]
        xb[k, x] = total
        x_copies[k] = [
            send(xb.at[k, x], xb.at[k, x], xx_s.at[k, o - 1], xx_r.at[k, o - 1], to_x(o)) for o in range(1, NX)
        ]

    def stage_x(k):
        for copy in x_copies[k]:
            copy.wait_recv()
        total = xb[k, 0]
        for i in range(1, NX):
            total = total + xb[k, i]
        lr[own_z(k), :] = split_columns(total * scale)
        block = lr.at[own_z(k)]
        za_copies[k] = [
            send(block, block, za_s.at[k, o - 1], za_r.at[k, o - 1], to_z(o)) for o in range(1, nz)
        ]

    def gather_z(k):
        for copy in za_copies[k]:
            copy.wait_recv()
        block = lr.at[own_y(k)]
        ya_copies[k] = [
            send(block, block, ya_s.at[k, o - 1], ya_r.at[k, o - 1], to_y(o)) for o in range(1, NY)
        ]

    def gather_y(k):
        for copy in ya_copies[k]:
            copy.wait_recv()
        block = lr.at[mine(k * hc, hc)]
        da_copies[k] = send(block, block, da_s.at[k], da_r.at[k], sib)

    def gather_core(k):
        da_copies[k].wait_recv()
        tile = min(512, hc)
        for h in range(2):
            @pl.loop(0, hc // tile)
            def _(i):
                row = pl.multiple_of(h * half + k * hc + i * tile, tile)
                pair = lr[pl.ds(row, tile), :]
                both = rows_dot(pair, e[pl.ds(row, tile), :])
                yt[...] += both[:RANK] + both[RANK:]
                u[...] += dot(xg[t, :, pl.ds(row, tile)], pair)
                square = rows_dot(pair, pair)
                gram[...] += (square[:RANK, :RANK] + square[RANK:, RANK:]) + (square[:RANK, RANK:] + square[RANK:, :RANK])

    yt[...] = jnp.zeros_like(yt)
    u[...] = jnp.zeros_like(u)
    gram[...] = jnp.zeros_like(gram)
    stages = (feed_core, feed_y, stage_y, stage_z, stage_x, gather_z, gather_y, gather_core)
    lags = (0, 1, 3, 4, 5, 6, 7, 8)
    for s in range(NCH + lags[-1]):
        for stage, lag in zip(stages, lags):
            if 0 <= s - lag < NCH:
                stage(s - lag)
                pump()
    pump(len(todo))

    lane = lax.broadcasted_iota(jnp.int32, (RANK, 2 * RANK), 1)
    sub = lax.broadcasted_iota(jnp.int32, (RANK, 2 * RANK), 0)
    aug[:, :RANK] = gram[...]
    aug[:, RANK:] = jnp.where(
        lax.broadcasted_iota(jnp.int32, (RANK, RANK), 0) == lax.broadcasted_iota(jnp.int32, (RANK, RANK), 1), 1.0, 0.0)

    def eliminate(first, last):
        @pl.loop(first, last)
        def _(j):
            row = aug[pl.ds(j, 1), :]
            pivot = jnp.sum(jnp.where(lane[:1] == j, row, 0.0), axis=1, keepdims=True)
            column = jnp.sum(jnp.where(lane == j, aug[...], 0.0), axis=1, keepdims=True)
            factor = jnp.where(sub[:, :1] > j, column / pivot, 0.0)
            aug[...] = aug[...] - factor * row

    ub[c, x] = u[:, :RANK] + u[:, RANK:]
    copies = [send(ub.at[c, x], ub.at[c, x], u_s.at[o], u_r.at[o], to_x(o)) for o in range(1, NX)]
    cuts = (0, RANK // 4, RANK // 2, 3 * RANK // 4, RANK)
    eliminate(cuts[0], cuts[1])
    for j in range(12):
        distant(j)
    for copy in copies:
        copy.wait_recv()
    u_copy = send(ub.at[c], ub.at[c], u_s.at[0], u_r.at[0], sib)
    for j in range(0, 3):
        multiply(j)
    u_copy.wait_recv()
    for core in range(2):
        for chip in range(NX):
            token = (chip * 2 + core) * tok
            both = rows_dot(split_columns(ub[core, chip]), g[token:token + tok, :])
            yt[...] += both[:RANK] + both[RANK:]

    part = RANK // NY
    own = pl.ds(pl.multiple_of(y * part, part), part)
    copies = [
        send(yt.at[pl.ds(pl.multiple_of(at_y(o) * part, part), part)], yb2.at[o - 1], q_s.at[0, o], q_r.at[0, o], to_y(o))
        for o in range(1, NY)
    ]
    for j in range(3, 6):
        multiply(j)
    eliminate(cuts[1], cuts[2])
    for copy in copies:
        copy.wait_recv()
    total = yt[own, :]
    for i in range(NY - 1):
        total = total + yb2[i]
    yy[z] = total
    copies = [send(yy.at[z], yy.at[z], q_s.at[1, o], q_r.at[1, o], to_z(o)) for o in range(1, nz)]
    eliminate(cuts[2], cuts[3])
    for j in range(6, 10):
        multiply(j)
    for copy in copies:
        copy.wait_recv()
    total = yy[0]
    for i in range(1, nz):
        total = total + yy[i]
    yr[own, :] = total * scale
    copies = [send(yr.at[own], yr.at[own], q_s.at[2, o], q_r.at[2, o], to_y(o)) for o in range(1, NY)]
    eliminate(cuts[3], cuts[4])
    pivots = jnp.sum(jnp.where(lane == sub, aug[...], 0.0), axis=1, keepdims=True)
    inverse = aug[:, RANK:] / jnp.sqrt(pivots)
    for copy in copies:
        copy.wait_recv()
    bt = dot(inverse, yr[...], precision=lax.Precision.HIGHEST)
    bt_ref[...] = bt
    wt_ref[...] = rows_dot(inverse, bt, precision=lax.Precision.HIGHEST)
    for j in range(12, XCH):
        distant(j)
    for j in range(10, XCH):
        multiply(j)
    for copy in sent:
        copy.wait_send()


def finish(merged, lr, wt, bt, rebuilt_ref, error_hbm, basis_ref, out, sems):
    dp = lax.axis_index("dp")
    width = merged.shape[0]
    share = rebuilt_ref.shape[0]
    high, low = split(wt[...])
    twice = jnp.concatenate([high, high], axis=0)

    def rebuild(pair):
        return dot(pair, twice) + dot(pair[:, :RANK], low)

    block = width // OUT
    tile = min(256, block)
    copies = []
    for j in range(OUT):
        @pl.loop(0, block // tile)
        def _(i):
            row = pl.multiple_of(j * block + i * tile, tile)
            rows = pl.ds(row, tile)
            out[rows, :] = (merged[rows, :] - rebuild(lr[rows, :])).astype(bf16)

        rows = pl.ds(j * block, block)
        copy = pltpu.make_async_copy(out.at[rows], error_hbm.at[0, rows], sems.at[j])
        copy.start()
        copies.append(copy)
    rebuilt_ref[...] = rebuild(lr[pl.ds(pl.multiple_of(dp * share, share), share), :]).astype(bf16)
    basis_ref[...] = bt[...].T
    for copy in copies:
        copy.wait()


def shards(inputs, out_grads, error_in, basis_in):
    replicas = lax.axis_size("dp")
    nz = replicas // NY
    tok, width = inputs.shape
    tokens, cols = out_grads.shape
    half = width // 2
    hc = half // NCH
    ybl = hc // NY
    zbl = ybl // nz
    scratch = [
        ((2 * NX, tok, width), bf16),
        ((tokens, cols), bf16),
        ((width, cols), bf16),
        ((width, RANK), f32),
        ((half, RANK), f32),
        ((NCH, NY - 1, ybl, RANK), f32),
        ((NCH, nz - 1, zbl, RANK), f32),
        ((NCH, NX, zbl, RANK), f32),
        ((2, NX, tok, RANK), f32),
        ((NX, tok, RANK), f32),
        ((NX - 1, tok, RANK), f32),
        ((cols, 2 * RANK), bf16),
        ((tok, 2 * RANK), bf16),
        ((tok, 2 * RANK), f32),
        ((2, NX, tok, RANK), f32),
        ((RANK, cols), f32),
        ((NY - 1, RANK // NY, cols), f32),
        ((nz, RANK // NY, cols), f32),
        ((RANK, cols), f32),
        ((RANK, RANK), f32),
        ((RANK, 2 * RANK), f32),
    ]
    sems = [
        (3,), (NX,), (NX,), (XCH, 2), (XCH, 2), (XCH, 2), (XCH, 2), (XCH + 1, 3), (XCH + 1, 3),
        (NCH,), (NCH,), (NCH, NY - 1), (NCH, NY - 1), (NCH, nz - 1), (NCH, nz - 1), (NCH, NX - 1), (NCH, NX - 1),
        (NCH, nz - 1), (NCH, nz - 1), (NCH, NY - 1), (NCH, NY - 1), (NCH,), (NCH,),
        (NX,), (NX,), (3, nz), (3, nz),
    ]
    anywhere = pl.BlockSpec(memory_space=pl.ANY)
    vmem = pl.BlockSpec(memory_space=pltpu.VMEM)
    merged, lr, wt, bt = pl.pallas_call(
        functools.partial(exchange, nz, 1.0 / replicas),
        out_shape=(
            pltpu.VMEM((width, cols), f32),
            pltpu.VMEM((width, 2 * RANK), bf16),
            pltpu.VMEM((RANK, cols), f32),
            pltpu.VMEM((RANK, cols), f32),
        ),
        in_specs=[anywhere, anywhere, anywhere, vmem],
        out_specs=(vmem,) * 4,
        scratch_shapes=[pltpu.VMEM(s, d) for s, d in scratch] + [pltpu.SemaphoreType.DMA(s) for s in sems],
        compiler_params=pltpu.CompilerParams(
            collective_id=0, has_side_effects=True, vmem_limit_bytes=42 * 2**20),
        name="exchange",
    )(inputs, out_grads, error_in[0], basis_in)

    share = width // replicas
    rebuilt, error_out, basis = pl.pallas_call(
        finish,
        out_shape=(
            jax.ShapeDtypeStruct((share, cols), bf16),
            jax.ShapeDtypeStruct((1, width, cols), bf16),
            jax.ShapeDtypeStruct((cols, RANK), f32),
        ),
        in_specs=[vmem] * 4,
        out_specs=(vmem, anywhere, vmem),
        scratch_shapes=[pltpu.VMEM((width, cols), bf16), pltpu.SemaphoreType.DMA((OUT,))],
        compiler_params=pltpu.CompilerParams(vmem_limit_bytes=12 * 2**20),
        name="finish",
    )(merged, lr, wt, bt)
    return rebuilt, error_out, basis


def solution(mesh):
    placed = (
        P(("dp", "tensor"), None),
        P("dp", "tensor"),
        P("dp", None, "tensor"),
        P("tensor", None),
    )
    return jax.shard_map(
        shards,
        mesh=mesh,
        in_specs=placed,
        out_specs=(P("dp", "tensor"), P("dp", None, "tensor"), P("tensor", None)),
        check_vma=False,
    )
```

```python
import functools

import jax
import jax.numpy as jnp
from jax import lax
from jax.experimental import pallas as pl
from jax.experimental.pallas import tpu as pltpu
from jax.sharding import PartitionSpec as P

NX = 4
NY = 4
RANK = 128
NCH = 4
XCH = 16
Z_FIRST = ()
LAG = 6
FAR, FULL = 4, 6
PUMP0, PUMP1 = 1, 1
OUT = 8
f32, bf16 = jnp.float32, jnp.bfloat16
MESH = pl.DeviceIdType.MESH
OVER_ROWS = (((0,), (0,)), ((), ()))


def timetable():
    lags = (0, 1, 3, 4, 5, 6, 7, 8)
    return [
        (stage, step - lag)
        for step in range(NCH + lags[-1]) for stage, lag in enumerate(lags) if 0 <= step - lag < NCH
    ]


def split(value):
    high = value.astype(bf16)
    return high, (value - high.astype(f32)).astype(bf16)


def split_columns(value):
    return jnp.concatenate(split(value), axis=1)


def rows_dot(left, right, **kw):
    return lax.dot_general(left, right, OVER_ROWS, preferred_element_type=f32, **kw)


def dot(left, right, **kw):
    return jnp.dot(left, right, preferred_element_type=f32, **kw)


def exchange(
    nz, scale,
    x_hbm, g_hbm, e_hbm, basis,
    merged, lr, wt_ref, bt_ref,
    xg, g, e, p, d2d, yb, zb, xb,
    gb, gbd, gbx, bhl, gbhl,
    u, ub, yt, yb2, yy, yr, gram, aug,
    local, gb_s, gb_r, x_s, x_r, f_s, f_r, sib_s, sib_r,
    d_s, d_r, y_s, y_r, z_s, z_r, xx_s, xx_r,
    za_s, za_r, ya_s, ya_r, da_s, da_r,
    u_s, u_r, q_s, q_r,
):
    width = x_hbm.shape[1]
    tok = x_hbm.shape[0]
    cols = e.shape[1]
    half = width // 2
    hc = half // NCH
    ybl = hc // NY
    zbl = ybl // nz
    cw = width // XCH
    dp = lax.axis_index("dp")
    t = lax.axis_index("tensor")
    z, y = dp // NY, dp % NY
    x, c = t // 2, t % 2
    sib = (dp, x * 2 + (1 - c))

    def at_x(o):
        return lax.rem(x + o + NX, NX)

    def to_x(o):
        return (dp, at_x(o) * 2 + c)

    def at_y(o):
        return lax.rem(y + o, NY)

    def to_y(o):
        return (z * NY + at_y(o), t)

    def at_z(o):
        return lax.rem(z + o, nz)

    def to_z(o):
        return (at_z(o) * NY + y, t)

    sent = []

    def send(src, dst, send_sem, recv_sem, device):
        copy = pltpu.make_async_remote_copy(
            src_ref=src, dst_ref=dst, send_sem=send_sem, recv_sem=recv_sem,
            device_id=device, device_id_type=MESH,
        )
        copy.start()
        sent.append(copy)
        return copy

    load_g = pltpu.make_async_copy(g_hbm, g, local.at[0])
    load_x = pltpu.make_async_copy(x_hbm, xg.at[t], local.at[1])
    load_e = pltpu.make_async_copy(e_hbm, e, local.at[2])
    load_g.start()
    load_x.start()
    load_e.start()

    barrier = pltpu.get_barrier_semaphore()
    partners = [sib] + [to_x(o) for o in range(1, NX)] + [to_y(o) for o in range(1, NY)] + [to_z(o) for o in range(1, nz)]
    for device in partners:
        pl.semaphore_signal(barrier, inc=1, device_id=device, device_id_type=MESH)

    bhl[...] = split_columns(basis[...])
    load_g.wait()
    for block in range(2 * NX):
        product = dot(g[block * tok:(block + 1) * tok, :], bhl[...])
        gb[block % 2, block // 2] = product[:, :RANK] + product[:, RANK:]
    pl.semaphore_wait(barrier, len(partners))
    gb_copy = send(gb.at[1 - c], gbd, gb_s.at[0], gb_r.at[0], sib)
    load_x.wait()

    def chunk_of(shard, j):
        return xg.at[shard, :, pl.ds(j * cw, cw)]

    def own_chunk(j):
        ring.append([
            send(chunk_of(t, j), chunk_of(t, j), x_s.at[j, i], x_r.at[j, i], to_x(o))
            for i, o in enumerate((1, -1))
        ])

    ring = []
    far = [None] * XCH
    to_sib = [[] for _ in range(XCH)]

    def near(j):
        ring[j][0].wait_recv()
        ring[j][1].wait_recv()
        left = chunk_of(at_x(-1) * 2 + c, j)
        right = chunk_of(at_x(1) * 2 + c, j)
        first, last = pl.ds(0, tok // 2), pl.ds(tok // 2, tok // 2)
        far[j] = [
            send(left.at[first], left.at[first], f_s.at[j, 0], f_r.at[j, 0], to_x(1)),
            send(right.at[last], right.at[last], f_s.at[j, 1], f_r.at[j, 1], to_x(-1)),
        ]
        to_sib[j].append(send(left, left, sib_s.at[j, 0], sib_r.at[j, 0], sib))
        to_sib[j].append(send(right, right, sib_s.at[j, 1], sib_r.at[j, 1], sib))

    def distant(j):
        for copy in far[j]:
            copy.wait_recv()
        block = chunk_of(at_x(2) * 2 + c, j)
        to_sib[j].append(send(block, block, sib_s.at[j, 2], sib_r.at[j, 2], sib))

    def multiply(j):
        if j == 0:
            own_sib.wait_recv()
        for copy in to_sib[j]:
            copy.wait_recv()
        tile = min(256, cw)

        @pl.loop(0, cw // tile)
        def _(i):
            row = pl.multiple_of(j * cw + i * tile, tile)
            block = xg[:, :, pl.ds(row, tile)].reshape(2 * NX * tok, tile)
            merged[pl.ds(row, tile), :] = rows_dot(block, g[...]) + e[pl.ds(row, tile), :].astype(f32)

    def forward(j):
        if j >= FAR:
            distant(j - FAR)
        near(j)
        if j >= FULL:
            multiply(j - FULL)

    todo = []
    for j in range(XCH + LAG):
        if j < XCH:
            todo.append(functools.partial(own_chunk, j))
        if j >= LAG:
            todo.append(functools.partial(forward, j - LAG))

    def pump(count=1):
        for _ in range(count):
            if todo:
                todo.pop(0)()

    pump(PUMP0)
    gb_copy.wait_recv()
    gb[c] = gb[c] + gbd[...]
    gb_copies = [
        send(gb.at[c, at_x(o)], gbx.at[o - 1], gb_s.at[o], gb_r.at[o], to_x(o)) for o in range(1, NX)
    ]

    own_sib = send(xg.at[t], xg.at[t], sib_s.at[XCH, 0], sib_r.at[XCH, 0], sib)
    pump(PUMP1)

    load_e.wait()
    base = min(512, width)

    @pl.loop(0, width // base)
    def _(i):
        row = pl.multiple_of(i * base, base)
        total = dot(e[pl.ds(row, base), :], bhl[...])
        p[pl.ds(row, base), :] = total[:, :RANK] + total[:, RANK:]

    for copy in gb_copies:
        copy.wait_recv()
    gbhl[...] = split_columns(gb[c, x] + gbx[0] + gbx[1] + gbx[2])

    def partial(h, k):
        tile = min(512, hc)

        @pl.loop(0, hc // tile)
        def _(i):
            at = pl.multiple_of(k * hc + i * tile, tile)
            row = pl.multiple_of(h * half + at, tile)
            total = rows_dot(xg[t, :, pl.ds(row, tile)], gbhl[...])
            p[pl.ds(row, tile), :] += total[:, :RANK] + total[:, RANK:]

    def mine(start, size):
        return pl.ds(pl.multiple_of(c * half + start, size), size)

    def theirs(start, size):
        return pl.ds(pl.multiple_of((1 - c) * half + start, size), size)

    y_copies, z_copies, x_copies = {}, {}, {}
    za_copies, ya_copies, da_copies = {}, {}, {}
    d_copies = {}

    def feed_core(k):
        partial(1 - c, k)
        d_copies[k] = send(p.at[theirs(k * hc, hc)], d2d.at[pl.ds(k * hc, hc)], d_s.at[k], d_r.at[k], sib)
        partial(c, k)

    over_y = (NY, to_y, at_y, y)
    over_z = (nz, to_z, at_z, z)

    def axes(k):
        return (over_z, over_y) if k in Z_FIRST else (over_y, over_z)

    def first_block(k, index):
        size = hc // axes(k)[0][0]
        return mine(k * hc + index * size, size)

    def second_block(k, index):
        (n1, _, _, own1), (n2, _, _, _) = axes(k)
        size = hc // n1 // n2
        return mine(k * hc + own1 * (hc // n1) + index * size, size)

    def own_first(k):
        return first_block(k, axes(k)[0][3])

    def own_second(k):
        return second_block(k, axes(k)[1][3])

    def feed_first(k):
        d_copies[k].wait_recv()
        p[mine(k * hc, hc), :] += d2d[pl.ds(k * hc, hc), :]
        n, to, at, _ = axes(k)[0]
        size = hc // n
        y_copies[k] = [
            send(p.at[first_block(k, at(o))], yb.at[k, pl.ds((o - 1) * size, size)], y_s.at[k, o - 1], y_r.at[k, o - 1], to(o))
            for o in range(1, n)
        ]

    def stage_first(k):
        for copy in y_copies[k]:
            copy.wait_recv()
        n, to, at, _ = axes(k)[0]
        size = hc // n
        total = p[own_first(k), :]
        for i in range(n - 1):
            total = total + yb[k, i * size:(i + 1) * size, :]
        p[own_first(k), :] = total
        n, to, at, _ = axes(k)[1]
        size = zbl
        z_copies[k] = [
            send(p.at[second_block(k, at(o))], zb.at[k, pl.ds((o - 1) * size, size)], z_s.at[k, o - 1], z_r.at[k, o - 1], to(o))
            for o in range(1, n)
        ]

    def stage_second(k):
        for copy in z_copies[k]:
            copy.wait_recv()
        total = p[own_second(k), :]
        for i in range(axes(k)[1][0] - 1):
            total = total + zb[k, i * zbl:(i + 1) * zbl, :]
        xb[k, x] = total
        x_copies[k] = [
            send(xb.at[k, x], xb.at[k, x], xx_s.at[k, o - 1], xx_r.at[k, o - 1], to_x(o)) for o in range(1, NX)
        ]

    def stage_x(k):
        for copy in x_copies[k]:
            copy.wait_recv()
        total = xb[k, 0]
        for i in range(1, NX):
            total = total + xb[k, i]
        lr[own_second(k), :] = split_columns(total * scale)
        block = lr.at[own_second(k)]
        n, to, _, _ = axes(k)[1]
        za_copies[k] = [
            send(block, block, za_s.at[k, o - 1], za_r.at[k, o - 1], to(o)) for o in range(1, n)
        ]

    def gather_second(k):
        for copy in za_copies[k]:
            copy.wait_recv()
        block = lr.at[own_first(k)]
        n, to, _, _ = axes(k)[0]
        ya_copies[k] = [
            send(block, block, ya_s.at[k, o - 1], ya_r.at[k, o - 1], to(o)) for o in range(1, n)
        ]

    def gather_first(k):
        for copy in ya_copies[k]:
            copy.wait_recv()
        block = lr.at[mine(k * hc, hc)]
        da_copies[k] = send(block, block, da_s.at[k], da_r.at[k], sib)

    def gather_core(k):
        da_copies[k].wait_recv()
        tile = min(512, hc)
        for h in range(2):
            @pl.loop(0, hc // tile)
            def _(i):
                row = pl.multiple_of(h * half + k * hc + i * tile, tile)
                pair = lr[pl.ds(row, tile), :]
                both = rows_dot(pair, e[pl.ds(row, tile), :])
                yt[...] += both[:RANK] + both[RANK:]
                u[...] += dot(xg[t, :, pl.ds(row, tile)], pair)
                square = rows_dot(pair, pair)
                gram[...] += (square[:RANK, :RANK] + square[RANK:, RANK:]) + (square[:RANK, RANK:] + square[RANK:, :RANK])

    yt[...] = jnp.zeros_like(yt)
    u[...] = jnp.zeros_like(u)
    gram[...] = jnp.zeros_like(gram)
    stages = (feed_core, feed_first, stage_first, stage_second, stage_x, gather_second, gather_first, gather_core)
    for stage, k in timetable():
        stages[stage](k)
        pump()
    pump(len(todo))

    lane = lax.broadcasted_iota(jnp.int32, (RANK, 2 * RANK), 1)
    sub = lax.broadcasted_iota(jnp.int32, (RANK, 2 * RANK), 0)
    aug[:, :RANK] = gram[...]
    aug[:, RANK:] = jnp.where(
        lax.broadcasted_iota(jnp.int32, (RANK, RANK), 0) == lax.broadcasted_iota(jnp.int32, (RANK, RANK), 1), 1.0, 0.0)

    def eliminate(first, last):
        @pl.loop(first, last)
        def _(j):
            row = aug[pl.ds(j, 1), :]
            pivot = jnp.sum(jnp.where(lane[:1] == j, row, 0.0), axis=1, keepdims=True)
            column = jnp.sum(jnp.where(lane == j, aug[...], 0.0), axis=1, keepdims=True)
            factor = jnp.where(sub[:, :1] > j, column / pivot, 0.0)
            aug[...] = aug[...] - factor * row

    ub[c, x] = u[:, :RANK] + u[:, RANK:]
    copies = [send(ub.at[c, x], ub.at[c, x], u_s.at[o], u_r.at[o], to_x(o)) for o in range(1, NX)]
    cuts = (0, RANK // 4, RANK // 2, 3 * RANK // 4, RANK)
    eliminate(cuts[0], cuts[1])
    rest = list(range(XCH - FULL, XCH))
    for j in range(XCH - FAR, XCH - 2):
        distant(j)
    multiply(rest.pop(0))
    for copy in copies:
        copy.wait_recv()
    u_copy = send(ub.at[c], ub.at[c], u_s.at[0], u_r.at[0], sib)
    multiply(rest.pop(0))
    u_copy.wait_recv()
    for core in range(2):
        for chip in range(NX):
            token = (chip * 2 + core) * tok
            both = rows_dot(split_columns(ub[core, chip]), g[token:token + tok, :])
            yt[...] += both[:RANK] + both[RANK:]

    part = RANK // NY
    own = pl.ds(pl.multiple_of(y * part, part), part)
    copies = [
        send(yt.at[pl.ds(pl.multiple_of(at_y(o) * part, part), part)], yb2.at[o - 1], q_s.at[0, o], q_r.at[0, o], to_y(o))
        for o in range(1, NY)
    ]
    eliminate(cuts[1], cuts[2])
    for j in range(XCH - 2, XCH):
        distant(j)
    for copy in copies:
        copy.wait_recv()
    total = yt[own, :]
    for i in range(NY - 1):
        total = total + yb2[i]
    yy[z] = total
    copies = [send(yy.at[z], yy.at[z], q_s.at[1, o], q_r.at[1, o], to_z(o)) for o in range(1, nz)]
    eliminate(cuts[2], cuts[3])
    multiply(rest.pop(0))
    multiply(rest.pop(0))
    for copy in copies:
        copy.wait_recv()
    total = yy[0]
    for i in range(1, nz):
        total = total + yy[i]
    yr[own, :] = total * scale
    copies = [send(yr.at[own], yr.at[own], q_s.at[2, o], q_r.at[2, o], to_y(o)) for o in range(1, NY)]
    eliminate(cuts[3], cuts[4])
    pivots = jnp.sum(jnp.where(lane == sub, aug[...], 0.0), axis=1, keepdims=True)
    inverse = aug[:, RANK:] / jnp.sqrt(pivots)
    for copy in copies:
        copy.wait_recv()
    bt = dot(inverse, yr[...], precision=lax.Precision.HIGHEST)
    bt_ref[...] = bt
    wt_ref[...] = rows_dot(inverse, bt, precision=lax.Precision.HIGHEST)
    for j in rest:
        multiply(j)
    for copy in sent:
        copy.wait_send()


def finish(merged, lr, wt, bt, rebuilt_ref, error_hbm, basis_ref, out, sems):
    dp = lax.axis_index("dp")
    width = merged.shape[0]
    share = rebuilt_ref.shape[0]
    high, low = split(wt[...])
    twice = jnp.concatenate([high, high], axis=0)

    def rebuild(pair):
        return dot(pair, twice) + dot(pair[:, :RANK], low)

    block = width // OUT
    tile = min(512, block)
    copies = []
    for j in range(OUT):
        @pl.loop(0, block // tile)
        def _(i):
            row = pl.multiple_of(j * block + i * tile, tile)
            rows = pl.ds(row, tile)
            out[rows, :] = (merged[rows, :] - rebuild(lr[rows, :])).astype(bf16)

        rows = pl.ds(j * block, block)
        copy = pltpu.make_async_copy(out.at[rows], error_hbm.at[0, rows], sems.at[j])
        copy.start()
        copies.append(copy)
    rebuilt_ref[...] = rebuild(lr[pl.ds(pl.multiple_of(dp * share, share), share), :]).astype(bf16)
    basis_ref[...] = bt[...].T
    for copy in copies:
        copy.wait()


def shards(inputs, out_grads, error_in, basis_in):
    replicas = lax.axis_size("dp")
    nz = replicas // NY
    tok, width = inputs.shape
    tokens, cols = out_grads.shape
    half = width // 2
    hc = half // NCH
    ybl = hc // NY
    zbl = ybl // nz
    scratch = [
        ((2 * NX, tok, width), bf16),
        ((tokens, cols), bf16),
        ((width, cols), bf16),
        ((width, RANK), f32),
        ((half, RANK), f32),
        ((NCH, hc, RANK), f32),
        ((NCH, hc // NY, RANK), f32),
        ((NCH, NX, zbl, RANK), f32),
        ((2, NX, tok, RANK), f32),
        ((NX, tok, RANK), f32),
        ((NX - 1, tok, RANK), f32),
        ((cols, 2 * RANK), bf16),
        ((tok, 2 * RANK), bf16),
        ((tok, 2 * RANK), f32),
        ((2, NX, tok, RANK), f32),
        ((RANK, cols), f32),
        ((NY - 1, RANK // NY, cols), f32),
        ((nz, RANK // NY, cols), f32),
        ((RANK, cols), f32),
        ((RANK, RANK), f32),
        ((RANK, 2 * RANK), f32),
    ]
    sems = [
        (3,), (NX,), (NX,), (XCH, 2), (XCH, 2), (XCH, 2), (XCH, 2), (XCH + 1, 3), (XCH + 1, 3),
        (NCH,), (NCH,), (NCH, nz - 1), (NCH, nz - 1), (NCH, nz - 1), (NCH, nz - 1), (NCH, NX - 1), (NCH, NX - 1),
        (NCH, nz - 1), (NCH, nz - 1), (NCH, nz - 1), (NCH, nz - 1), (NCH,), (NCH,),
        (NX,), (NX,), (3, nz), (3, nz),
    ]
    anywhere = pl.BlockSpec(memory_space=pl.ANY)
    vmem = pl.BlockSpec(memory_space=pltpu.VMEM)
    merged, lr, wt, bt = pl.pallas_call(
        functools.partial(exchange, nz, 1.0 / replicas),
        out_shape=(
            pltpu.VMEM((width, cols), f32),
            pltpu.VMEM((width, 2 * RANK), bf16),
            pltpu.VMEM((RANK, cols), f32),
            pltpu.VMEM((RANK, cols), f32),
        ),
        in_specs=[anywhere, anywhere, anywhere, vmem],
        out_specs=(vmem,) * 4,
        scratch_shapes=[pltpu.VMEM(s, d) for s, d in scratch] + [pltpu.SemaphoreType.DMA(s) for s in sems],
        compiler_params=pltpu.CompilerParams(
            collective_id=0, has_side_effects=True, vmem_limit_bytes=42 * 2**20),
        name="exchange",
    )(inputs, out_grads, error_in[0], basis_in)

    share = width // replicas
    rebuilt, error_out, basis = pl.pallas_call(
        finish,
        out_shape=(
            jax.ShapeDtypeStruct((share, cols), bf16),
            jax.ShapeDtypeStruct((1, width, cols), bf16),
            jax.ShapeDtypeStruct((cols, RANK), f32),
        ),
        in_specs=[vmem] * 4,
        out_specs=(vmem, anywhere, vmem),
        scratch_shapes=[pltpu.VMEM((width, cols), bf16), pltpu.SemaphoreType.DMA((OUT,))],
        compiler_params=pltpu.CompilerParams(vmem_limit_bytes=12 * 2**20),
        name="finish",
    )(merged, lr, wt, bt)
    return rebuilt, error_out, basis


def solution(mesh):
    placed = (
        P(("dp", "tensor"), None),
        P("dp", "tensor"),
        P("dp", None, "tensor"),
        P("tensor", None),
    )
    return jax.shard_map(
        shards,
        mesh=mesh,
        in_specs=placed,
        out_specs=(P("dp", "tensor"), P("dp", None, "tensor"), P("tensor", None)),
        check_vma=False,
    )
```

```python
import functools

import jax
import jax.numpy as jnp
from jax import lax
from jax.experimental import pallas as pl
from jax.experimental.pallas import tpu as pltpu
from jax.sharding import PartitionSpec as P

NX = 4
NY = 4
RANK = 128
NCH = 4
XCH = 16
Z_FIRST = ()
LAG = 6
FAR, FULL = 4, 6
PUMP0, PUMP1 = 1, 1
PUMPS = (2, 2, 2, 3, 3, 3, 3, 3, 3, 3, 3, 3)
OUT = 8
f32, bf16 = jnp.float32, jnp.bfloat16
MESH = pl.DeviceIdType.MESH
OVER_ROWS = (((0,), (0,)), ((), ()))


def split(value):
    high = value.astype(bf16)
    return high, (value - high.astype(f32)).astype(bf16)


def split_columns(value):
    return jnp.concatenate(split(value), axis=1)


def rows_dot(left, right, **kw):
    return lax.dot_general(left, right, OVER_ROWS, preferred_element_type=f32, **kw)


def dot(left, right, **kw):
    return jnp.dot(left, right, preferred_element_type=f32, **kw)


def exchange(
    nz, scale,
    x_hbm, g_hbm, e_hbm, basis,
    merged, lr, wt_ref, bt_ref,
    xg, g, e, p, d2d, yb, zb, xb,
    gb, gbd, gbx, bhl, gbhl,
    u, ub, yt, yb2, yy, yr, gram, aug,
    local, gb_s, gb_r, x_s, x_r, f_s, f_r, sib_s, sib_r,
    d_s, d_r, y_s, y_r, z_s, z_r, xx_s, xx_r,
    za_s, za_r, ya_s, ya_r, da_s, da_r,
    u_s, u_r, q_s, q_r,
):
    width = x_hbm.shape[1]
    tok = x_hbm.shape[0]
    cols = e.shape[1]
    half = width // 2
    hc = half // NCH
    ybl = hc // NY
    zbl = ybl // nz
    cw = width // XCH
    dp = lax.axis_index("dp")
    t = lax.axis_index("tensor")
    z, y = dp // NY, dp % NY
    x, c = t // 2, t % 2
    sib = (dp, x * 2 + (1 - c))

    def at_x(o):
        return lax.rem(x + o + NX, NX)

    def to_x(o):
        return (dp, at_x(o) * 2 + c)

    def at_y(o):
        return lax.rem(y + o, NY)

    def to_y(o):
        return (z * NY + at_y(o), t)

    def at_z(o):
        return lax.rem(z + o, nz)

    def to_z(o):
        return (at_z(o) * NY + y, t)

    sent = []

    def send(src, dst, send_sem, recv_sem, device):
        copy = pltpu.make_async_remote_copy(
            src_ref=src, dst_ref=dst, send_sem=send_sem, recv_sem=recv_sem,
            device_id=device, device_id_type=MESH,
        )
        copy.start()
        sent.append(copy)
        return copy

    load_g = pltpu.make_async_copy(g_hbm, g, local.at[0])
    load_x = pltpu.make_async_copy(x_hbm, xg.at[t], local.at[1])
    load_e = pltpu.make_async_copy(e_hbm, e, local.at[2])
    load_g.start()
    load_x.start()
    load_e.start()

    barrier = pltpu.get_barrier_semaphore()
    partners = [sib] + [to_x(o) for o in range(1, NX)] + [to_y(o) for o in range(1, NY)] + [to_z(o) for o in range(1, nz)]
    for device in partners:
        pl.semaphore_signal(barrier, inc=1, device_id=device, device_id_type=MESH)

    bhl[...] = split_columns(basis[...])
    load_g.wait()
    for block in range(2 * NX):
        product = dot(g[block * tok:(block + 1) * tok, :], bhl[...])
        gb[block % 2, block // 2] = product[:, :RANK] + product[:, RANK:]
    pl.semaphore_wait(barrier, len(partners))
    gb_copy = send(gb.at[1 - c], gbd, gb_s.at[0], gb_r.at[0], sib)
    load_x.wait()

    def chunk_of(shard, j):
        return xg.at[shard, :, pl.ds(j * cw, cw)]

    def own_chunk(j):
        ring.append([
            send(chunk_of(t, j), chunk_of(t, j), x_s.at[j, i], x_r.at[j, i], to_x(o))
            for i, o in enumerate((1, -1))
        ])

    ring = []
    far = [None] * XCH
    to_sib = [[] for _ in range(XCH)]

    def near(j):
        ring[j][0].wait_recv()
        ring[j][1].wait_recv()
        left = chunk_of(at_x(-1) * 2 + c, j)
        right = chunk_of(at_x(1) * 2 + c, j)
        first, last = pl.ds(0, tok // 2), pl.ds(tok // 2, tok // 2)
        far[j] = [
            send(left.at[first], left.at[first], f_s.at[j, 0], f_r.at[j, 0], to_x(1)),
            send(right.at[last], right.at[last], f_s.at[j, 1], f_r.at[j, 1], to_x(-1)),
        ]
        to_sib[j].append(send(left, left, sib_s.at[j, 0], sib_r.at[j, 0], sib))
        to_sib[j].append(send(right, right, sib_s.at[j, 1], sib_r.at[j, 1], sib))

    def distant(j):
        for copy in far[j]:
            copy.wait_recv()
        block = chunk_of(at_x(2) * 2 + c, j)
        to_sib[j].append(send(block, block, sib_s.at[j, 2], sib_r.at[j, 2], sib))

    def multiply(j):
        if j == 0:
            own_sib.wait_recv()
        for copy in to_sib[j]:
            copy.wait_recv()
        tile = min(512, cw)

        @pl.loop(0, cw // tile)
        def _(i):
            row = pl.multiple_of(j * cw + i * tile, tile)
            block = xg[:, :, pl.ds(row, tile)].reshape(2 * NX * tok, tile)
            merged[pl.ds(row, tile), :] = rows_dot(block, g[...]) + e[pl.ds(row, tile), :].astype(f32)

    def forward(j):
        if j >= FAR:
            distant(j - FAR)
        near(j)
        if j >= FULL:
            multiply(j - FULL)

    todo = []
    for j in range(XCH + LAG):
        if j < XCH:
            todo.append(functools.partial(own_chunk, j))
        if j >= LAG:
            todo.append(functools.partial(forward, j - LAG))

    def pump(count=1):
        for _ in range(count):
            if todo:
                todo.pop(0)()

    pump(PUMP0)
    gb_copy.wait_recv()
    gb[c] = gb[c] + gbd[...]
    gb_copies = [
        send(gb.at[c, at_x(o)], gbx.at[o - 1], gb_s.at[o], gb_r.at[o], to_x(o)) for o in range(1, NX)
    ]

    own_sib = send(xg.at[t], xg.at[t], sib_s.at[XCH, 0], sib_r.at[XCH, 0], sib)
    pump(PUMP1)

    load_e.wait()
    base = min(512, width)

    @pl.loop(0, width // base)
    def _(i):
        row = pl.multiple_of(i * base, base)
        total = dot(e[pl.ds(row, base), :], bhl[...])
        p[pl.ds(row, base), :] = total[:, :RANK] + total[:, RANK:]

    for copy in gb_copies:
        copy.wait_recv()
    gbhl[...] = split_columns(gb[c, x] + gbx[0] + gbx[1] + gbx[2])

    def partial(h, k):
        tile = min(512, hc)

        @pl.loop(0, hc // tile)
        def _(i):
            at = pl.multiple_of(k * hc + i * tile, tile)
            row = pl.multiple_of(h * half + at, tile)
            total = rows_dot(xg[t, :, pl.ds(row, tile)], gbhl[...])
            p[pl.ds(row, tile), :] += total[:, :RANK] + total[:, RANK:]

    def mine(start, size):
        return pl.ds(pl.multiple_of(c * half + start, size), size)

    def theirs(start, size):
        return pl.ds(pl.multiple_of((1 - c) * half + start, size), size)

    y_copies, z_copies, x_copies = {}, {}, {}
    za_copies, ya_copies, da_copies = {}, {}, {}
    d_copies = {}

    def feed_core(k):
        partial(1 - c, k)
        d_copies[k] = send(p.at[theirs(k * hc, hc)], d2d.at[pl.ds(k * hc, hc)], d_s.at[k], d_r.at[k], sib)
        partial(c, k)

    over_y = (NY, to_y, at_y, y)
    over_z = (nz, to_z, at_z, z)

    def axes(k):
        return (over_z, over_y) if k in Z_FIRST else (over_y, over_z)

    def first_block(k, index):
        size = hc // axes(k)[0][0]
        return mine(k * hc + index * size, size)

    def second_block(k, index):
        (n1, _, _, own1), (n2, _, _, _) = axes(k)
        size = hc // n1 // n2
        return mine(k * hc + own1 * (hc // n1) + index * size, size)

    def own_first(k):
        return first_block(k, axes(k)[0][3])

    def own_second(k):
        return second_block(k, axes(k)[1][3])

    def feed_first(k):
        d_copies[k].wait_recv()
        p[mine(k * hc, hc), :] += d2d[pl.ds(k * hc, hc), :]
        n, to, at, _ = axes(k)[0]
        size = hc // n
        y_copies[k] = [
            send(p.at[first_block(k, at(o))], yb.at[k, pl.ds((o - 1) * size, size)], y_s.at[k, o - 1], y_r.at[k, o - 1], to(o))
            for o in range(1, n)
        ]

    def stage_first(k):
        for copy in y_copies[k]:
            copy.wait_recv()
        n, to, at, _ = axes(k)[0]
        size = hc // n
        total = p[own_first(k), :]
        for i in range(n - 1):
            total = total + yb[k, i * size:(i + 1) * size, :]
        p[own_first(k), :] = total
        n, to, at, _ = axes(k)[1]
        size = zbl
        z_copies[k] = [
            send(p.at[second_block(k, at(o))], zb.at[k, pl.ds((o - 1) * size, size)], z_s.at[k, o - 1], z_r.at[k, o - 1], to(o))
            for o in range(1, n)
        ]

    def stage_second(k):
        for copy in z_copies[k]:
            copy.wait_recv()
        total = p[own_second(k), :]
        for i in range(axes(k)[1][0] - 1):
            total = total + zb[k, i * zbl:(i + 1) * zbl, :]
        xb[k, x] = total
        x_copies[k] = [
            send(xb.at[k, x], xb.at[k, x], xx_s.at[k, o - 1], xx_r.at[k, o - 1], to_x(o)) for o in range(1, NX)
        ]

    def stage_x(k):
        for copy in x_copies[k]:
            copy.wait_recv()
        total = xb[k, 0]
        for i in range(1, NX):
            total = total + xb[k, i]
        lr[own_second(k), :] = split_columns(total * scale)
        block = lr.at[own_second(k)]
        n, to, _, _ = axes(k)[1]
        za_copies[k] = [
            send(block, block, za_s.at[k, o - 1], za_r.at[k, o - 1], to(o)) for o in range(1, n)
        ]

    def gather_second(k):
        for copy in za_copies[k]:
            copy.wait_recv()
        block = lr.at[own_first(k)]
        n, to, _, _ = axes(k)[0]
        ya_copies[k] = [
            send(block, block, ya_s.at[k, o - 1], ya_r.at[k, o - 1], to(o)) for o in range(1, n)
        ]

    def gather_first(k):
        for copy in ya_copies[k]:
            copy.wait_recv()
        block = lr.at[mine(k * hc, hc)]
        da_copies[k] = send(block, block, da_s.at[k], da_r.at[k], sib)

    def gather_core(k):
        da_copies[k].wait_recv()
        tile = min(512, hc)
        for h in range(2):
            @pl.loop(0, hc // tile)
            def _(i):
                row = pl.multiple_of(h * half + k * hc + i * tile, tile)
                pair = lr[pl.ds(row, tile), :]
                both = rows_dot(pair, e[pl.ds(row, tile), :])
                yt[...] += both[:RANK] + both[RANK:]
                u[...] += dot(xg[t, :, pl.ds(row, tile)], pair)
                square = rows_dot(pair, pair)
                gram[...] += (square[:RANK, :RANK] + square[RANK:, RANK:]) + (square[:RANK, RANK:] + square[RANK:, :RANK])

    yt[...] = jnp.zeros_like(yt)
    u[...] = jnp.zeros_like(u)
    gram[...] = jnp.zeros_like(gram)
    stages = (feed_core, feed_first, stage_first, stage_second, stage_x, gather_second, gather_first, gather_core)
    lags = (0, 1, 3, 4, 5, 6, 7, 8)
    for s in range(NCH + lags[-1]):
        for stage, lag in tuple(zip(stages, lags))[::-1]:
            if 0 <= s - lag < NCH:
                stage(s - lag)
        pump(PUMPS[s])
    pump(len(todo))

    lane = lax.broadcasted_iota(jnp.int32, (RANK, 2 * RANK), 1)
    sub = lax.broadcasted_iota(jnp.int32, (RANK, 2 * RANK), 0)
    aug[:, :RANK] = gram[...]
    aug[:, RANK:] = jnp.where(
        lax.broadcasted_iota(jnp.int32, (RANK, RANK), 0) == lax.broadcasted_iota(jnp.int32, (RANK, RANK), 1), 1.0, 0.0)

    def eliminate(first, last):
        @pl.loop(first, last)
        def _(j):
            row = aug[pl.ds(j, 1), :]
            pivot = jnp.sum(jnp.where(lane[:1, :RANK] == j, row[:, :RANK], 0.0), axis=1, keepdims=True)
            column = jnp.sum(jnp.where(lane[:, :RANK] == j, aug[:, :RANK], 0.0), axis=1, keepdims=True)
            factor = jnp.where(sub[:, :1] > j, column / pivot, 0.0)
            aug[...] = aug[...] - factor * row

    early = list(sent)

    def finished(shares):
        for _ in range(-(-len(early) // shares)):
            early.pop(0).wait_send()

    last = len(sent)
    ub[c, x] = u[:, :RANK] + u[:, RANK:]
    copies = [send(ub.at[c, x], ub.at[c, x], u_s.at[o], u_r.at[o], to_x(o)) for o in range(1, NX)]
    cuts = (0, RANK // 4, RANK // 2, 3 * RANK // 4, RANK)
    eliminate(cuts[0], cuts[1])
    rest = list(range(XCH - FULL, XCH))
    for j in range(XCH - FAR, XCH - 2):
        distant(j)
    multiply(rest.pop(0))
    for copy in copies:
        copy.wait_recv()
    u_copy = send(ub.at[c], ub.at[c], u_s.at[0], u_r.at[0], sib)
    finished(3)
    multiply(rest.pop(0))
    u_copy.wait_recv()
    for core in range(2):
        for chip in range(NX):
            token = (chip * 2 + core) * tok
            both = rows_dot(split_columns(ub[core, chip]), g[token:token + tok, :])
            yt[...] += both[:RANK] + both[RANK:]

    part = RANK // NY
    own = pl.ds(pl.multiple_of(y * part, part), part)
    copies = [
        send(yt.at[pl.ds(pl.multiple_of(at_y(o) * part, part), part)], yb2.at[o - 1], q_s.at[0, o], q_r.at[0, o], to_y(o))
        for o in range(1, NY)
    ]
    finished(2)
    eliminate(cuts[1], cuts[2])
    for j in range(XCH - 2, XCH):
        distant(j)
    for copy in copies:
        copy.wait_recv()
    total = yt[own, :]
    for i in range(NY - 1):
        total = total + yb2[i]
    yy[z] = total
    copies = [send(yy.at[z], yy.at[z], q_s.at[1, o], q_r.at[1, o], to_z(o)) for o in range(1, nz)]
    finished(1)
    eliminate(cuts[2], cuts[3])
    multiply(rest.pop(0))
    multiply(rest.pop(0))
    for copy in copies:
        copy.wait_recv()
    total = yy[0]
    for i in range(1, nz):
        total = total + yy[i]
    yr[own, :] = total * scale
    copies = [send(yr.at[own], yr.at[own], q_s.at[2, o], q_r.at[2, o], to_y(o)) for o in range(1, NY)]
    eliminate(cuts[3], cuts[4])
    pivots = jnp.sum(jnp.where(lane == sub, aug[...], 0.0), axis=1, keepdims=True)
    inverse = aug[:, RANK:] / jnp.sqrt(pivots)
    for copy in copies:
        copy.wait_recv()
    bt = dot(inverse, yr[...], precision=lax.Precision.HIGHEST)
    bt_ref[...] = bt
    wt_ref[...] = rows_dot(inverse, bt, precision=lax.Precision.HIGHEST)
    for j in rest:
        multiply(j)
    for copy in early + sent[last:]:
        copy.wait_send()


def finish(merged, lr, wt, bt, rebuilt_ref, error_hbm, basis_ref, out, sems):
    dp = lax.axis_index("dp")
    width = merged.shape[0]
    share = rebuilt_ref.shape[0]
    high, low = split(wt[...])
    twice = jnp.concatenate([high, high], axis=0)

    def rebuild(pair):
        return dot(pair, twice) + dot(pair[:, :RANK], low)

    block = width // OUT
    tile = min(512, block)
    copies = []
    for j in range(OUT):
        @pl.loop(0, block // tile)
        def _(i):
            row = pl.multiple_of(j * block + i * tile, tile)
            rows = pl.ds(row, tile)
            out[rows, :] = (merged[rows, :] - rebuild(lr[rows, :])).astype(bf16)

        rows = pl.ds(j * block, block)
        copy = pltpu.make_async_copy(out.at[rows], error_hbm.at[0, rows], sems.at[j])
        copy.start()
        copies.append(copy)
    rebuilt_ref[...] = rebuild(lr[pl.ds(pl.multiple_of(dp * share, share), share), :]).astype(bf16)
    basis_ref[...] = bt[...].T
    for copy in copies:
        copy.wait()


def shards(inputs, out_grads, error_in, basis_in):
    replicas = lax.axis_size("dp")
    nz = replicas // NY
    tok, width = inputs.shape
    tokens, cols = out_grads.shape
    half = width // 2
    hc = half // NCH
    ybl = hc // NY
    zbl = ybl // nz
    scratch = [
        ((2 * NX, tok, width), bf16),
        ((tokens, cols), bf16),
        ((width, cols), bf16),
        ((width, RANK), f32),
        ((half, RANK), f32),
        ((NCH, hc, RANK), f32),
        ((NCH, hc // NY, RANK), f32),
        ((NCH, NX, zbl, RANK), f32),
        ((2, NX, tok, RANK), f32),
        ((NX, tok, RANK), f32),
        ((NX - 1, tok, RANK), f32),
        ((cols, 2 * RANK), bf16),
        ((tok, 2 * RANK), bf16),
        ((tok, 2 * RANK), f32),
        ((2, NX, tok, RANK), f32),
        ((RANK, cols), f32),
        ((NY - 1, RANK // NY, cols), f32),
        ((nz, RANK // NY, cols), f32),
        ((RANK, cols), f32),
        ((RANK, RANK), f32),
        ((RANK, 2 * RANK), f32),
    ]
    sems = [
        (3,), (NX,), (NX,), (XCH, 2), (XCH, 2), (XCH, 2), (XCH, 2), (XCH + 1, 3), (XCH + 1, 3),
        (NCH,), (NCH,), (NCH, nz - 1), (NCH, nz - 1), (NCH, nz - 1), (NCH, nz - 1), (NCH, NX - 1), (NCH, NX - 1),
        (NCH, nz - 1), (NCH, nz - 1), (NCH, nz - 1), (NCH, nz - 1), (NCH,), (NCH,),
        (NX,), (NX,), (3, nz), (3, nz),
    ]
    anywhere = pl.BlockSpec(memory_space=pl.ANY)
    vmem = pl.BlockSpec(memory_space=pltpu.VMEM)
    merged, lr, wt, bt = pl.pallas_call(
        functools.partial(exchange, nz, 1.0 / replicas),
        out_shape=(
            pltpu.VMEM((width, cols), f32),
            pltpu.VMEM((width, 2 * RANK), bf16),
            pltpu.VMEM((RANK, cols), f32),
            pltpu.VMEM((RANK, cols), f32),
        ),
        in_specs=[anywhere, anywhere, anywhere, vmem],
        out_specs=(vmem,) * 4,
        scratch_shapes=[pltpu.VMEM(s, d) for s, d in scratch] + [pltpu.SemaphoreType.DMA(s) for s in sems],
        compiler_params=pltpu.CompilerParams(
            collective_id=0, has_side_effects=True, vmem_limit_bytes=42 * 2**20),
        name="exchange",
    )(inputs, out_grads, error_in[0], basis_in)

    share = width // replicas
    rebuilt, error_out, basis = pl.pallas_call(
        finish,
        out_shape=(
            jax.ShapeDtypeStruct((share, cols), bf16),
            jax.ShapeDtypeStruct((1, width, cols), bf16),
            jax.ShapeDtypeStruct((cols, RANK), f32),
        ),
        in_specs=[vmem] * 4,
        out_specs=(vmem, anywhere, vmem),
        scratch_shapes=[pltpu.VMEM((width, cols), bf16), pltpu.SemaphoreType.DMA((OUT,))],
        compiler_params=pltpu.CompilerParams(vmem_limit_bytes=12 * 2**20),
        name="finish",
    )(merged, lr, wt, bt)
    return rebuilt, error_out, basis


def solution(mesh):
    placed = (
        P(("dp", "tensor"), None),
        P("dp", "tensor"),
        P("dp", None, "tensor"),
        P("tensor", None),
    )
    return jax.shard_map(
        shards,
        mesh=mesh,
        in_specs=placed,
        out_specs=(P("dp", "tensor"), P("dp", None, "tensor"), P("tensor", None)),
        check_vma=False,
    )
```

```python
import functools

import jax
import jax.numpy as jnp
from jax import lax
from jax.experimental import pallas as pl
from jax.experimental.pallas import tpu as pltpu
from jax.sharding import PartitionSpec as P

NX = 4
NY = 4
RANK = 128
NCH = 4
XCH = 16
Z_FIRST = ()
LAG = 6
FAR, FULL = 4, 6
PUMP0, PUMP1 = 1, 1
PUMPS = (2, 2, 2, 3, 3, 3, 3, 3, 3, 3, 3, 3)
OUT = 8
f32, bf16 = jnp.float32, jnp.bfloat16
MESH = pl.DeviceIdType.MESH
OVER_ROWS = (((0,), (0,)), ((), ()))


def split(value):
    high = value.astype(bf16)
    return high, (value - high.astype(f32)).astype(bf16)


def split_columns(value):
    return jnp.concatenate(split(value), axis=1)


def rows_dot(left, right, **kw):
    return lax.dot_general(left, right, OVER_ROWS, preferred_element_type=f32, **kw)


def dot(left, right, **kw):
    return jnp.dot(left, right, preferred_element_type=f32, **kw)


def exchange(
    nz, scale,
    x_hbm, g_hbm, e_hbm, basis,
    merged, lr, wt_ref, bt_ref,
    xg, g, e, p, d2d, yb, zb, xb,
    gb, gbd, gbx, bhl, gbhl,
    u, ub, yt, yb2, yy, yr, gram, aug,
    local, gb_s, gb_r, x_s, x_r, f_s, f_r, sib_s, sib_r,
    d_s, d_r, y_s, y_r, z_s, z_r, xx_s, xx_r,
    za_s, za_r, ya_s, ya_r, da_s, da_r,
    u_s, u_r, q_s, q_r,
):
    width = x_hbm.shape[1]
    tok = x_hbm.shape[0]
    cols = e.shape[1]
    half = width // 2
    hc = half // NCH
    ybl = hc // NY
    zbl = ybl // nz
    cw = width // XCH
    dp = lax.axis_index("dp")
    t = lax.axis_index("tensor")
    z, y = dp // NY, dp % NY
    x, c = t // 2, t % 2
    sib = (dp, x * 2 + (1 - c))

    def at_x(o):
        return lax.rem(x + o + NX, NX)

    def to_x(o):
        return (dp, at_x(o) * 2 + c)

    def at_y(o):
        return lax.rem(y + o, NY)

    def to_y(o):
        return (z * NY + at_y(o), t)

    def at_z(o):
        return lax.rem(z + o, nz)

    def to_z(o):
        return (at_z(o) * NY + y, t)

    sent = []

    def send(src, dst, send_sem, recv_sem, device):
        copy = pltpu.make_async_remote_copy(
            src_ref=src, dst_ref=dst, send_sem=send_sem, recv_sem=recv_sem,
            device_id=device, device_id_type=MESH,
        )
        copy.start()
        sent.append(copy)
        return copy

    load_g = pltpu.make_async_copy(g_hbm, g, local.at[0])
    load_x = pltpu.make_async_copy(x_hbm, xg.at[t], local.at[1])
    load_e = pltpu.make_async_copy(e_hbm, e, local.at[2])
    load_g.start()
    load_x.start()
    load_e.start()

    barrier = pltpu.get_barrier_semaphore()
    partners = [sib] + [to_x(o) for o in range(1, NX)] + [to_y(o) for o in range(1, NY)] + [to_z(o) for o in range(1, nz)]
    for device in partners:
        pl.semaphore_signal(barrier, inc=1, device_id=device, device_id_type=MESH)

    bhl[...] = split_columns(basis[...])
    load_g.wait()
    for block in range(2 * NX):
        product = dot(g[block * tok:(block + 1) * tok, :], bhl[...])
        gb[block % 2, block // 2] = product[:, :RANK] + product[:, RANK:]
    pl.semaphore_wait(barrier, len(partners))
    gb_copy = send(gb.at[1 - c], gbd, gb_s.at[0], gb_r.at[0], sib)
    load_x.wait()

    def chunk_of(shard, j):
        return xg.at[shard, :, pl.ds(j * cw, cw)]

    def own_chunk(j):
        ring.append([
            send(chunk_of(t, j), chunk_of(t, j), x_s.at[j, i], x_r.at[j, i], to_x(o))
            for i, o in enumerate((1, -1))
        ])

    ring = []
    far = [None] * XCH
    to_sib = [[] for _ in range(XCH)]

    def near(j):
        ring[j][0].wait_recv()
        ring[j][1].wait_recv()
        left = chunk_of(at_x(-1) * 2 + c, j)
        right = chunk_of(at_x(1) * 2 + c, j)
        first, last = pl.ds(0, tok // 2), pl.ds(tok // 2, tok // 2)
        far[j] = [
            send(left.at[first], left.at[first], f_s.at[j, 0], f_r.at[j, 0], to_x(1)),
            send(right.at[last], right.at[last], f_s.at[j, 1], f_r.at[j, 1], to_x(-1)),
        ]
        to_sib[j].append(send(left, left, sib_s.at[j, 0], sib_r.at[j, 0], sib))
        to_sib[j].append(send(right, right, sib_s.at[j, 1], sib_r.at[j, 1], sib))

    def distant(j):
        for copy in far[j]:
            copy.wait_recv()
        block = chunk_of(at_x(2) * 2 + c, j)
        to_sib[j].append(send(block, block, sib_s.at[j, 2], sib_r.at[j, 2], sib))

    def multiply(j):
        if j == 0:
            own_sib.wait_recv()
        for copy in to_sib[j]:
            copy.wait_recv()
        tile = min(512, cw)

        @pl.loop(0, cw // tile)
        def _(i):
            row = pl.multiple_of(j * cw + i * tile, tile)
            block = xg[:, :, pl.ds(row, tile)].reshape(2 * NX * tok, tile)
            merged[pl.ds(row, tile), :] = rows_dot(block, g[...]) + e[pl.ds(row, tile), :].astype(f32)

    def forward(j):
        if j >= FAR:
            distant(j - FAR)
        near(j)
        if j >= FULL:
            multiply(j - FULL)

    todo = []
    for j in range(XCH + LAG):
        if j < XCH:
            todo.append(functools.partial(own_chunk, j))
        if j >= LAG:
            todo.append(functools.partial(forward, j - LAG))

    def pump(count=1):
        for _ in range(count):
            if todo:
                todo.pop(0)()

    pump(PUMP0)
    gb_copy.wait_recv()
    gb[c] = gb[c] + gbd[...]
    gb_copies = [
        send(gb.at[c, at_x(o)], gbx.at[o - 1], gb_s.at[o], gb_r.at[o], to_x(o)) for o in range(1, NX)
    ]

    own_sib = send(xg.at[t], xg.at[t], sib_s.at[XCH, 0], sib_r.at[XCH, 0], sib)
    pump(PUMP1)

    load_e.wait()
    base = min(1024, width)

    @pl.loop(0, width // base)
    def _(i):
        row = pl.multiple_of(i * base, base)
        total = dot(e[pl.ds(row, base), :], bhl[...])
        p[pl.ds(row, base), :] = total[:, :RANK] + total[:, RANK:]

    for copy in gb_copies:
        copy.wait_recv()
    gbhl[...] = split_columns(gb[c, x] + gbx[0] + gbx[1] + gbx[2])

    def partial(h, k):
        tile = min(1024, hc)

        @pl.loop(0, hc // tile)
        def _(i):
            at = pl.multiple_of(k * hc + i * tile, tile)
            row = pl.multiple_of(h * half + at, tile)
            total = rows_dot(xg[t, :, pl.ds(row, tile)], gbhl[...])
            p[pl.ds(row, tile), :] += total[:, :RANK] + total[:, RANK:]

    def mine(start, size):
        return pl.ds(pl.multiple_of(c * half + start, size), size)

    def theirs(start, size):
        return pl.ds(pl.multiple_of((1 - c) * half + start, size), size)

    y_copies, z_copies, x_copies = {}, {}, {}
    za_copies, ya_copies, da_copies = {}, {}, {}
    d_copies = {}

    def feed_core(k):
        partial(1 - c, k)
        d_copies[k] = send(p.at[theirs(k * hc, hc)], d2d.at[pl.ds(k * hc, hc)], d_s.at[k], d_r.at[k], sib)
        partial(c, k)

    over_y = (NY, to_y, at_y, y)
    over_z = (nz, to_z, at_z, z)

    def axes(k):
        return (over_z, over_y) if k in Z_FIRST else (over_y, over_z)

    def first_block(k, index):
        size = hc // axes(k)[0][0]
        return mine(k * hc + index * size, size)

    def second_block(k, index):
        (n1, _, _, own1), (n2, _, _, _) = axes(k)
        size = hc // n1 // n2
        return mine(k * hc + own1 * (hc // n1) + index * size, size)

    def own_first(k):
        return first_block(k, axes(k)[0][3])

    def own_second(k):
        return second_block(k, axes(k)[1][3])

    def feed_first(k):
        d_copies[k].wait_recv()
        p[mine(k * hc, hc), :] += d2d[pl.ds(k * hc, hc), :]
        n, to, at, _ = axes(k)[0]
        size = hc // n
        y_copies[k] = [
            send(p.at[first_block(k, at(o))], yb.at[k, pl.ds((o - 1) * size, size)], y_s.at[k, o - 1], y_r.at[k, o - 1], to(o))
            for o in range(1, n)
        ]

    def stage_first(k):
        for copy in y_copies[k]:
            copy.wait_recv()
        n, to, at, _ = axes(k)[0]
        size = hc // n
        total = p[own_first(k), :]
        for i in range(n - 1):
            total = total + yb[k, i * size:(i + 1) * size, :]
        p[own_first(k), :] = total
        n, to, at, _ = axes(k)[1]
        size = zbl
        z_copies[k] = [
            send(p.at[second_block(k, at(o))], zb.at[k, pl.ds((o - 1) * size, size)], z_s.at[k, o - 1], z_r.at[k, o - 1], to(o))
            for o in range(1, n)
        ]

    def stage_second(k):
        for copy in z_copies[k]:
            copy.wait_recv()
        total = p[own_second(k), :]
        for i in range(axes(k)[1][0] - 1):
            total = total + zb[k, i * zbl:(i + 1) * zbl, :]
        xb[k, x] = total
        x_copies[k] = [
            send(xb.at[k, x], xb.at[k, x], xx_s.at[k, o - 1], xx_r.at[k, o - 1], to_x(o)) for o in range(1, NX)
        ]

    def stage_x(k):
        for copy in x_copies[k]:
            copy.wait_recv()
        total = xb[k, 0]
        for i in range(1, NX):
            total = total + xb[k, i]
        lr[own_second(k), :] = split_columns(total * scale)
        block = lr.at[own_second(k)]
        n, to, _, _ = axes(k)[1]
        za_copies[k] = [
            send(block, block, za_s.at[k, o - 1], za_r.at[k, o - 1], to(o)) for o in range(1, n)
        ]

    def gather_second(k):
        for copy in za_copies[k]:
            copy.wait_recv()
        block = lr.at[own_first(k)]
        n, to, _, _ = axes(k)[0]
        ya_copies[k] = [
            send(block, block, ya_s.at[k, o - 1], ya_r.at[k, o - 1], to(o)) for o in range(1, n)
        ]

    def gather_first(k):
        for copy in ya_copies[k]:
            copy.wait_recv()
        block = lr.at[mine(k * hc, hc)]
        da_copies[k] = send(block, block, da_s.at[k], da_r.at[k], sib)

    def gather_core(k):
        da_copies[k].wait_recv()
        tile = min(1024, hc)
        for h in range(2):
            @pl.loop(0, hc // tile)
            def _(i):
                row = pl.multiple_of(h * half + k * hc + i * tile, tile)
                pair = lr[pl.ds(row, tile), :]
                both = rows_dot(pair, e[pl.ds(row, tile), :])
                yt[...] += both[:RANK] + both[RANK:]
                u[...] += dot(xg[t, :, pl.ds(row, tile)], pair)
                square = rows_dot(pair, pair)
                gram[...] += (square[:RANK, :RANK] + square[RANK:, RANK:]) + (square[:RANK, RANK:] + square[RANK:, :RANK])

    yt[...] = jnp.zeros_like(yt)
    u[...] = jnp.zeros_like(u)
    gram[...] = jnp.zeros_like(gram)
    stages = (feed_core, feed_first, stage_first, stage_second, stage_x, gather_second, gather_first, gather_core)
    lags = (0, 1, 3, 4, 5, 6, 7, 8)
    for s in range(NCH + lags[-1]):
        for stage, lag in tuple(zip(stages, lags))[::-1]:
            if 0 <= s - lag < NCH:
                stage(s - lag)
        pump(PUMPS[s])
    pump(len(todo))

    lane = lax.broadcasted_iota(jnp.int32, (RANK, 2 * RANK), 1)
    sub = lax.broadcasted_iota(jnp.int32, (RANK, 2 * RANK), 0)
    aug[:, :RANK] = gram[...]
    aug[:, RANK:] = jnp.where(
        lax.broadcasted_iota(jnp.int32, (RANK, RANK), 0) == lax.broadcasted_iota(jnp.int32, (RANK, RANK), 1), 1.0, 0.0)

    def eliminate(first, last):
        @pl.loop(first, last)
        def _(j):
            row = aug[pl.ds(j, 1), :]
            pivot = jnp.sum(jnp.where(lane[:1, :RANK] == j, row[:, :RANK], 0.0), axis=1, keepdims=True)
            column = jnp.sum(jnp.where(lane[:, :RANK] == j, aug[:, :RANK], 0.0), axis=1, keepdims=True)
            factor = jnp.where(sub[:, :1] > j, column / pivot, 0.0)
            aug[...] = aug[...] - factor * row

    early = list(sent)

    def finished(shares):
        for _ in range(-(-len(early) // shares)):
            early.pop(0).wait_send()

    last = len(sent)
    ub[c, x] = u[:, :RANK] + u[:, RANK:]
    copies = [send(ub.at[c, x], ub.at[c, x], u_s.at[o], u_r.at[o], to_x(o)) for o in range(1, NX)]
    cuts = (0, RANK // 4, RANK // 2, 3 * RANK // 4, RANK)
    eliminate(cuts[0], cuts[1])
    rest = list(range(XCH - FULL, XCH))
    for j in range(XCH - FAR, XCH - 2):
        distant(j)
    multiply(rest.pop(0))
    for copy in copies:
        copy.wait_recv()
    u_copy = send(ub.at[c], ub.at[c], u_s.at[0], u_r.at[0], sib)
    finished(3)
    multiply(rest.pop(0))
    u_copy.wait_recv()
    for core in range(2):
        for chip in range(NX):
            token = (chip * 2 + core) * tok
            both = rows_dot(split_columns(ub[core, chip]), g[token:token + tok, :])
            yt[...] += both[:RANK] + both[RANK:]

    part = RANK // NY
    own = pl.ds(pl.multiple_of(y * part, part), part)
    copies = [
        send(yt.at[pl.ds(pl.multiple_of(at_y(o) * part, part), part)], yb2.at[o - 1], q_s.at[0, o], q_r.at[0, o], to_y(o))
        for o in range(1, NY)
    ]
    finished(2)
    eliminate(cuts[1], cuts[2])
    for j in range(XCH - 2, XCH):
        distant(j)
    for copy in copies:
        copy.wait_recv()
    total = yt[own, :]
    for i in range(NY - 1):
        total = total + yb2[i]
    yy[z] = total
    copies = [send(yy.at[z], yy.at[z], q_s.at[1, o], q_r.at[1, o], to_z(o)) for o in range(1, nz)]
    finished(1)
    eliminate(cuts[2], cuts[3])
    multiply(rest.pop(0))
    multiply(rest.pop(0))
    for copy in copies:
        copy.wait_recv()
    total = yy[0]
    for i in range(1, nz):
        total = total + yy[i]
    yr[own, :] = total * scale
    copies = [send(yr.at[own], yr.at[own], q_s.at[2, o], q_r.at[2, o], to_y(o)) for o in range(1, NY)]
    eliminate(cuts[3], cuts[4])
    pivots = jnp.sum(jnp.where(lane == sub, aug[...], 0.0), axis=1, keepdims=True)
    inverse = aug[:, RANK:] / jnp.sqrt(pivots)
    for copy in copies:
        copy.wait_recv()
    bt = dot(inverse, yr[...], precision=lax.Precision.HIGHEST)
    bt_ref[...] = bt
    wt_ref[...] = rows_dot(inverse, bt, precision=lax.Precision.HIGHEST)
    for j in rest:
        multiply(j)
    for copy in early + sent[last:]:
        copy.wait_send()


def finish(merged, lr, wt, bt, rebuilt_ref, error_hbm, basis_ref, out, sems):
    dp = lax.axis_index("dp")
    width = merged.shape[0]
    share = rebuilt_ref.shape[0]
    high, low = split(wt[...])
    twice = jnp.concatenate([high, high], axis=0)

    def rebuild(pair):
        return dot(pair, twice) + dot(pair[:, :RANK], low)

    block = width // OUT
    tile = min(512, block)
    copies = []
    for j in range(OUT):
        @pl.loop(0, block // tile)
        def _(i):
            row = pl.multiple_of(j * block + i * tile, tile)
            rows = pl.ds(row, tile)
            out[rows, :] = (merged[rows, :] - rebuild(lr[rows, :])).astype(bf16)

        rows = pl.ds(j * block, block)
        copy = pltpu.make_async_copy(out.at[rows], error_hbm.at[0, rows], sems.at[j])
        copy.start()
        copies.append(copy)
    rebuilt_ref[...] = rebuild(lr[pl.ds(pl.multiple_of(dp * share, share), share), :]).astype(bf16)
    basis_ref[...] = bt[...].T
    for copy in copies:
        copy.wait()


def shards(inputs, out_grads, error_in, basis_in):
    replicas = lax.axis_size("dp")
    nz = replicas // NY
    tok, width = inputs.shape
    tokens, cols = out_grads.shape
    half = width // 2
    hc = half // NCH
    ybl = hc // NY
    zbl = ybl // nz
    scratch = [
        ((2 * NX, tok, width), bf16),
        ((tokens, cols), bf16),
        ((width, cols), bf16),
        ((width, RANK), f32),
        ((half, RANK), f32),
        ((NCH, hc, RANK), f32),
        ((NCH, hc // NY, RANK), f32),
        ((NCH, NX, zbl, RANK), f32),
        ((2, NX, tok, RANK), f32),
        ((NX, tok, RANK), f32),
        ((NX - 1, tok, RANK), f32),
        ((cols, 2 * RANK), bf16),
        ((tok, 2 * RANK), bf16),
        ((tok, 2 * RANK), f32),
        ((2, NX, tok, RANK), f32),
        ((RANK, cols), f32),
        ((NY - 1, RANK // NY, cols), f32),
        ((nz, RANK // NY, cols), f32),
        ((RANK, cols), f32),
        ((RANK, RANK), f32),
        ((RANK, 2 * RANK), f32),
    ]
    sems = [
        (3,), (NX,), (NX,), (XCH, 2), (XCH, 2), (XCH, 2), (XCH, 2), (XCH + 1, 3), (XCH + 1, 3),
        (NCH,), (NCH,), (NCH, nz - 1), (NCH, nz - 1), (NCH, nz - 1), (NCH, nz - 1), (NCH, NX - 1), (NCH, NX - 1),
        (NCH, nz - 1), (NCH, nz - 1), (NCH, nz - 1), (NCH, nz - 1), (NCH,), (NCH,),
        (NX,), (NX,), (3, nz), (3, nz),
    ]
    anywhere = pl.BlockSpec(memory_space=pl.ANY)
    vmem = pl.BlockSpec(memory_space=pltpu.VMEM)
    merged, lr, wt, bt = pl.pallas_call(
        functools.partial(exchange, nz, 1.0 / replicas),
        out_shape=(
            pltpu.VMEM((width, cols), f32),
            pltpu.VMEM((width, 2 * RANK), bf16),
            pltpu.VMEM((RANK, cols), f32),
            pltpu.VMEM((RANK, cols), f32),
        ),
        in_specs=[anywhere, anywhere, anywhere, vmem],
        out_specs=(vmem,) * 4,
        scratch_shapes=[pltpu.VMEM(s, d) for s, d in scratch] + [pltpu.SemaphoreType.DMA(s) for s in sems],
        compiler_params=pltpu.CompilerParams(
            collective_id=0, has_side_effects=True, vmem_limit_bytes=42 * 2**20),
        name="exchange",
    )(inputs, out_grads, error_in[0], basis_in)

    share = width // replicas
    rebuilt, error_out, basis = pl.pallas_call(
        finish,
        out_shape=(
            jax.ShapeDtypeStruct((share, cols), bf16),
            jax.ShapeDtypeStruct((1, width, cols), bf16),
            jax.ShapeDtypeStruct((cols, RANK), f32),
        ),
        in_specs=[vmem] * 4,
        out_specs=(vmem, anywhere, vmem),
        scratch_shapes=[pltpu.VMEM((width, cols), bf16), pltpu.SemaphoreType.DMA((OUT,))],
        compiler_params=pltpu.CompilerParams(vmem_limit_bytes=12 * 2**20),
        name="finish",
    )(merged, lr, wt, bt)
    return rebuilt, error_out, basis


def solution(mesh):
    placed = (
        P(("dp", "tensor"), None),
        P("dp", "tensor"),
        P("dp", None, "tensor"),
        P("tensor", None),
    )
    return jax.shard_map(
        shards,
        mesh=mesh,
        in_specs=placed,
        out_specs=(P("dp", "tensor"), P("dp", None, "tensor"), P("tensor", None)),
        check_vma=False,
    )
```
